512 devices in a mesh: grp: 16 (over z, core), lev: 32 (over y, x).
Axes of the slice: x: 4, y: 8, z: 8, core: 2. Of those that a mesh axis runs over, the one named last changes fastest.
Arguments:
- ocean_field: bfloat16 [16, 64, 524288], P(None, 'lev', 'grp'), may hold values from -6 to 6
- climatology: float32 [64, 524288], P(None, ('grp', 'lev')), may hold values from -3 to 3
- land_mask: int32 [524288], P(('grp', 'lev')), may hold values 0 or 1
- bottom_index: int32 [524288], P(('grp', 'lev')), may hold values from 16 to 64
- vertical_modes: bfloat16 [16, 64], replicated, may hold values from -0.75 to 0.75
Outputs:
- factor: float32 [256, 256], replicated
- whitened: float32 [256, 524288], P(None, ('grp', 'lev'))
The draws below stay inside these ranges and needn't reach their ends.
All inputs are finite; a program needn't handle non-finite values. No bound on the sum of `land_mask` on one device may be relied on, other than what follows from the above.
Results may differ from the reference program's by a relative error of at most 0.008.
Values may be sent and summed in bfloat16 or wider, within the bound.
A program may use at most 128 MiB of HBM per device.

```python
import jax
import jax.numpy as jnp
from jax import lax

DAYS = 16
LEVELS = 64
MODES = 16
COLS = 524288


def with_ends(drawn, rng, low, largest):
    dims = drawn.shape
    place = [jax.random.randint(jax.random.fold_in(rng, axis), (), 0, dims[axis]) for axis in range(len(dims))]
    drawn = drawn.at[tuple(place)].set(low)
    longest = dims.index(max(dims))
    place[longest] = (place[longest] + 1) % dims[longest]
    return drawn.at[tuple(place)].set(largest)


def block_levels(key, shape, cuts, low, largest):
    def one(axis_at, blocks):
        draws = jax.random.uniform(jax.random.fold_in(jax.random.fold_in(key, 6), axis_at), (blocks,), jnp.float32, low / len(cuts), largest / len(cuts))
        return jnp.repeat(jnp.exp(draws), shape[axis_at] // blocks).reshape((-1,) + (1,) * (len(shape) - axis_at - 1))

    level = one(*cuts[0])
    for cut in cuts[1:]:
        level = level * one(*cut)
    return level


def bell_draw(key, extent, deviation, reach, pieces=(), kind=jnp.bfloat16):
    level = block_levels(key, extent, pieces, -0.22, 0.18) if pieces else 1.0
    result = jax.random.normal(key, extent, jnp.float32) * deviation * level
    return jnp.minimum(jnp.maximum(result, -reach), reach).astype(kind)


def setup_inputs(seed: int = 0) -> dict:
    arg_keys = jax.random.split(jax.random.key(seed), 6)
    return {
        "ocean_field": bell_draw(arg_keys[0], (DAYS, LEVELS, COLS), 1.0, 6.0, ((1, 32), (2, 16))),
        "climatology": bell_draw(arg_keys[1], (LEVELS, COLS), 0.5, 3.0, ((1, 512),), jnp.float32),
        "land_mask": with_ends((jax.random.randint(arg_keys[2], (COLS,), 0, 4) < 3).astype(jnp.int32), jax.random.fold_in(arg_keys[2], 1), 0, 1),
        "bottom_index": with_ends(jax.random.randint(arg_keys[3], (COLS,), LEVELS // 4, LEVELS + 1), jax.random.fold_in(arg_keys[3], 1), LEVELS // 4, LEVELS).astype(jnp.int32),
        "vertical_modes": bell_draw(arg_keys[4], (MODES, LEVELS), LEVELS ** -0.5, 0.75),
    }


def reference(ocean_field, climatology, land_mask, bottom_index, vertical_modes):
    level_ids = lax.broadcasted_iota(jnp.int32, (LEVELS, COLS), 0)
    water = jnp.where((level_ids < bottom_index[None, :]) & (land_mask[None, :] == 1), 1.0, 0.0).astype(jnp.float32)
    rows_list = []
    for day in range(DAYS):
        anomaly = ((ocean_field[day].astype(jnp.float32) - climatology) * water).astype(jnp.bfloat16)
        rows_list.append(jnp.dot(vertical_modes.astype(jnp.float32), anomaly.astype(jnp.float32), preferred_element_type=jnp.float32))
    stacked = jnp.concatenate(rows_list, axis=0)
    gram = jnp.dot(stacked, stacked.T, precision=lax.Precision.HIGHEST) / jnp.float32(COLS)
    factor = jnp.linalg.cholesky(gram).T
    whitened = jax.scipy.linalg.solve_triangular(factor.T, stacked, lower=True)
    return (factor, whitened)
```

```python
import functools

import jax
import jax.numpy as jnp
from jax import lax
from jax.experimental import pallas as pl
from jax.experimental.pallas import tpu as pltpu
from jax.sharding import PartitionSpec as P

MESH = pl.DeviceIdType.MESH
DAYS = 16
MODES = 16
LANES = 128


def exchange_kernel(
    n_grp, n_lev, total_cols,
    ocean_ref, clim_ref, mask_ref, bottom_ref, modes_ref,
    stacked_ref, gram_ref,
    recv, clim_rows, limit_rows, weights, anomaly, part, rs_buf, sum_buf, gather_buf,
    local_sem, a_send, a_recv, r_send, r_recv, s_send, s_recv, g_send, g_recv,
):
    me_g = lax.axis_index("grp")
    me_l = lax.axis_index("lev")
    slabs = clim_ref.shape[1] // LANES
    rows = 2 * slabs

    def lev_peer(o):
        return lax.rem(me_l + o, n_lev)

    def lev_from(o):
        return lax.rem(me_l + n_lev - o, n_lev)

    def grp_peer(o):
        return lax.rem(me_g + o, n_grp)

    def grp_from(o):
        return lax.rem(me_g + n_grp - o, n_grp)

    barrier = pltpu.get_barrier_semaphore()

    @pl.loop(1, n_lev)
    def _(o):
        pl.semaphore_signal(barrier, inc=1, device_id=(me_g, lev_peer(o)), device_id_type=MESH)

    @pl.loop(1, n_grp)
    def _(o):
        pl.semaphore_signal(barrier, inc=1, device_id=(grp_peer(o), me_l), device_id_type=MESH)

    pl.semaphore_wait(barrier, n_lev + n_grp - 2)

    def block_copy(to, slot, k):
        return pltpu.make_async_remote_copy(
            src_ref=ocean_ref.at[:, pl.ds(pl.multiple_of(to * rows, rows), rows), :],
            dst_ref=recv.at[slot],
            send_sem=a_send.at[k],
            recv_sem=a_recv.at[k],
            device_id=(me_g, to),
            device_id_type=MESH,
        )

    @pl.loop(1, n_lev)
    def _(o):
        block_copy(lev_peer(o), me_l, o).start()

    own = pltpu.make_async_copy(
        ocean_ref.at[:, pl.ds(pl.multiple_of(me_l * rows, rows), rows), :], recv.at[me_l], local_sem
    )
    own.start()

    limit = jnp.where(mask_ref[...] == 1, bottom_ref[...], 0)
    for slab in range(slabs):
        limit_rows[2 * slab : 2 * slab + 1, :] = limit[slab : slab + 1, :]
        limit_rows[2 * slab + 1 : 2 * slab + 2, :] = limit[slab : slab + 1, :] - 1

    @pl.loop(0, clim_ref.shape[0] // 8)
    def _(t):
        block = clim_ref[pl.ds(pl.multiple_of(t * 8, 8), 8), :]
        for k in range(8):
            for slab in range(slabs):
                row = 2 * slab + k % 2
                clim_rows[4 * t + k // 2, row : row + 1, :] = block[
                    k : k + 1, slab * LANES : (slab + 1) * LANES
                ]

    width = slabs * MODES
    depth = n_lev * rows
    levels = modes_ref.shape[1]
    r = lax.broadcasted_iota(jnp.int32, (width, MODES), 0)
    m = lax.broadcasted_iota(jnp.int32, (width, MODES), 1)
    spread_modes = jnp.where(lax.rem(r, MODES) == m, 1.0, 0.0).astype(jnp.bfloat16)
    l = lax.broadcasted_iota(jnp.int32, (levels, depth), 0)
    q = lax.broadcasted_iota(jnp.int32, (levels, depth), 1)
    spread_levels = jnp.where(2 * (q // rows) + lax.rem(q, 2) == l, 1.0, 0.0).astype(jnp.bfloat16)
    tall = jnp.dot(spread_modes, modes_ref[...], preferred_element_type=jnp.float32).astype(jnp.bfloat16)
    wide = jnp.dot(tall, spread_levels, preferred_element_type=jnp.float32)
    r = lax.broadcasted_iota(jnp.int32, (width, depth), 0)
    q = lax.broadcasted_iota(jnp.int32, (width, depth), 1)
    weights[...] = jnp.where(r // MODES == lax.rem(q, rows) // 2, wide, 0.0).astype(jnp.bfloat16)

    def use(s):
        water = limit_rows[...] > 2 * s
        clim = clim_rows[s]
        for d in range(DAYS):
            diff = recv[s, d].astype(jnp.float32) - clim
            anomaly[pl.ds(pl.multiple_of(s * rows, rows), rows), d * LANES : (d + 1) * LANES] = jnp.where(
                water, diff, 0.0
            ).astype(jnp.bfloat16)

    own.wait()
    use(me_l)

    @pl.loop(1, n_lev)
    def _(o):
        s = lev_from(o)
        block_copy(s, s, o).wait_recv()
        use(s)

    coef = jnp.dot(weights[...], anomaly[...], preferred_element_type=jnp.float32)
    for d in range(DAYS):
        for slab in range(slabs):
            stacked_ref[d * MODES : (d + 1) * MODES, slab * LANES : (slab + 1) * LANES] = coef[
                slab * MODES : (slab + 1) * MODES, d * LANES : (d + 1) * LANES
            ]
    stacked = stacked_ref[...]
    part[...] = lax.dot_general(
        stacked, stacked, (((1,), (1,)), ((), ())),
        precision=lax.Precision.HIGHEST, preferred_element_type=jnp.float32,
    )

    piece = part.shape[0] // n_lev

    def rows_of(i):
        return pl.ds(pl.multiple_of(i * piece, piece), piece)

    def scatter_copy(to, slot, k):
        return pltpu.make_async_remote_copy(
            src_ref=part.at[rows_of(to)], dst_ref=rs_buf.at[slot],
            send_sem=r_send.at[k], recv_sem=r_recv.at[k],
            device_id=(me_g, to), device_id_type=MESH,
        )

    @pl.loop(1, n_lev)
    def _(o):
        scatter_copy(lev_peer(o), me_l, o).start()

    rs_buf[me_l] = part[rows_of(me_l)]

    @pl.loop(1, n_lev)
    def _(o):
        s = lev_from(o)
        scatter_copy(s, s, o).wait_recv()

    sum_buf[me_g] = jnp.sum(rs_buf[...], axis=0)

    def sum_copy(to, slot, k):
        return pltpu.make_async_remote_copy(
            src_ref=sum_buf.at[me_g], dst_ref=sum_buf.at[slot],
            send_sem=s_send.at[k], recv_sem=s_recv.at[k],
            device_id=(to, me_l), device_id_type=MESH,
        )

    @pl.loop(1, n_grp)
    def _(o):
        sum_copy(grp_peer(o), me_g, o).start()

    @pl.loop(1, n_grp)
    def _(o):
        s = grp_from(o)
        sum_copy(s, s, o).wait_recv()

    gather_buf[me_l] = jnp.sum(sum_buf[...], axis=0) * (1.0 / total_cols)

    def gather_copy(to, slot, k):
        return pltpu.make_async_remote_copy(
            src_ref=gather_buf.at[me_l], dst_ref=gather_buf.at[slot],
            send_sem=g_send.at[k], recv_sem=g_recv.at[k],
            device_id=(me_g, to), device_id_type=MESH,
        )

    @pl.loop(1, n_lev)
    def _(o):
        gather_copy(lev_peer(o), me_l, o).start()

    gram_ref[rows_of(me_l)] = gather_buf[me_l]

    @pl.loop(1, n_lev)
    def _(o):
        s = lev_from(o)
        gather_copy(s, s, o).wait_recv()
        gram_ref[rows_of(s)] = gather_buf[s]

    @pl.loop(1, n_lev)
    def _(o):
        block_copy(lev_peer(o), me_l, o).wait_send()
        scatter_copy(lev_peer(o), me_l, o).wait_send()
        gather_copy(lev_peer(o), me_l, o).wait_send()

    @pl.loop(1, n_grp)
    def _(o):
        sum_copy(grp_peer(o), me_g, o).wait_send()


def exchange(n_grp, n_lev, ocean, climatology, land_mask, bottom_index, modes):
    days, levels_dev, cols_grp = ocean.shape
    col_dev = climatology.shape[1]
    slabs = col_dev // LANES
    rows = levels_dev * slabs
    total_cols = col_dev * n_grp * n_lev
    width = DAYS * MODES
    piece = width // n_lev
    tiles = cols_grp // LANES
    ocean = ocean.reshape(days, levels_dev, tiles, LANES).transpose(0, 2, 1, 3)
    ocean = ocean.reshape(days, tiles * levels_dev, LANES)
    vmem = pl.BlockSpec(memory_space=pltpu.VMEM)
    return pl.pallas_call(
        functools.partial(exchange_kernel, n_grp, n_lev, total_cols),
        out_shape=(
            jax.ShapeDtypeStruct((width, col_dev), jnp.float32),
            jax.ShapeDtypeStruct((width, width), jnp.float32),
        ),
        in_specs=[pl.BlockSpec(memory_space=pl.ANY)] + [vmem] * 4,
        out_specs=(vmem, vmem),
        scratch_shapes=[
            pltpu.VMEM((n_lev, days, rows, LANES), jnp.bfloat16),
            pltpu.VMEM((n_lev, rows, LANES), jnp.float32),
            pltpu.VMEM((rows, LANES), jnp.int32),
            pltpu.VMEM((slabs * MODES, n_lev * rows), jnp.bfloat16),
            pltpu.VMEM((n_lev * rows, days * LANES), jnp.bfloat16),
            pltpu.VMEM((width, width), jnp.float32),
            pltpu.VMEM((n_lev, piece, width), jnp.float32),
            pltpu.VMEM((n_grp, piece, width), jnp.float32),
            pltpu.VMEM((n_lev, piece, width), jnp.float32),
            pltpu.SemaphoreType.DMA,
        ]
        + [pltpu.SemaphoreType.DMA((n_lev,))] * 4
        + [pltpu.SemaphoreType.DMA((n_grp,))] * 2
        + [pltpu.SemaphoreType.DMA((n_lev,))] * 2,
        compiler_params=pltpu.CompilerParams(
            collective_id=0, has_side_effects=True, vmem_limit_bytes=40 * 1024 * 1024
        ),
        name="exchange",
    )(
        ocean, climatology,
        land_mask.reshape(slabs, LANES), bottom_index.reshape(slabs, LANES), modes,
    )


def mm(a, b, dims=((1,), (0,))):
    return lax.dot_general(a, b, (dims, ((), ())), precision=lax.Precision.HIGHEST, preferred_element_type=jnp.float32)


def eliminate(a):
    n = a.shape[0]
    w = 8
    lane = lax.broadcasted_iota(jnp.int32, (w, n), 1)
    sub = lax.broadcasted_iota(jnp.int32, (w, n), 0)
    rows = [a[w * h : w * h + w] for h in range(n // w)]

    def spread(x):
        return jnp.broadcast_to(x, (w, n))

    for g in range(n // w):
        at = g * w
        col = [spread(rows[g][:, at + k : at + k + 1]) for k in range(w)]
        row = rows[g]
        pivots, splats = [], []
        for k in range(w):
            inv = 1.0 / spread(col[k][k : k + 1])
            pivot = jnp.where(lane == at + k, inv, spread(row[k : k + 1]) * inv)
            pivots.append(jnp.where((lane > at + k) & (lane < at + w), 0.0, pivot))
            splats.append({j: spread(col[j][k : k + 1]) * inv for j in range(k + 1, w)})
            if k < w - 1:
                m = jnp.where(sub > k, col[k], 0.0)
                row = jnp.where((lane == at + k) & (sub > k), 0.0, row) - m * pivot
                for j in range(k + 1, w):
                    col[j] = col[j] - m * splats[k][j]
        rows[g] = row
        inside = (lane >= at) & (lane < at + w)
        for h in range(g + 1, n // w):
            c = [spread(rows[h][:, at + k : at + k + 1]) for k in range(w)]
            out = jnp.where(inside, 0.0, rows[h])
            for k in range(w):
                for j in range(k + 1, w):
                    c[j] = c[j] - c[k] * splats[k][j]
            for k in range(w):
                out = out - c[k] * pivots[k]
            rows[h] = out
    upper, inverse = [], []
    for h in range(n // w):
        at = sub + w * h
        scale = lax.rsqrt(spread(jnp.sum(jnp.where(lane == at, rows[h], 0.0), axis=1, keepdims=True)))
        upper.append(jnp.where(lane >= at, rows[h] * scale, 0.0))
        inverse.append(jnp.where(lane == at, scale, jnp.where(lane < at, rows[h] * scale, 0.0)))
    return jnp.concatenate(upper, axis=0), jnp.concatenate(inverse, axis=0)

def whiten_kernel(gram_ref, stacked_ref, factor_ref, whitened_ref):
    half = gram_ref.shape[0] // 2
    r11, i11 = eliminate(gram_ref[:half, :half])
    r12 = mm(i11, gram_ref[:half, half:])
    factor_ref[:half, :half] = r11
    factor_ref[:half, half:] = r12
    factor_ref[half:, :half] = jnp.zeros((half, half), jnp.float32)
    rest = gram_ref[half:, half:] - mm(r12, r12, ((0,), (0,)))
    first = mm(i11, stacked_ref[:half])
    whitened_ref[:half] = first
    left = stacked_ref[half:] - mm(r12, first, ((0,), (0,)))
    r22, i22 = eliminate(rest)
    factor_ref[half:, half:] = r22
    whitened_ref[half:] = mm(i22, left)


def whiten(gram, stacked):
    vmem = pl.BlockSpec(memory_space=pltpu.VMEM)
    return pl.pallas_call(
        whiten_kernel,
        out_shape=(
            jax.ShapeDtypeStruct(gram.shape, jnp.float32),
            jax.ShapeDtypeStruct(stacked.shape, jnp.float32),
        ),
        in_specs=[vmem, vmem],
        out_specs=(vmem, vmem),
        compiler_params=pltpu.CompilerParams(vmem_limit_bytes=40 * 1024 * 1024),
        name="whiten",
    )(gram, stacked)


def solution(mesh):
    n_grp, n_lev = mesh.shape["grp"], mesh.shape["lev"]

    def on_device(ocean_field, climatology, land_mask, bottom_index, vertical_modes):
        stacked, gram = exchange(
            n_grp, n_lev, ocean_field, climatology, land_mask, bottom_index, vertical_modes
        )
        return whiten(gram, stacked)

    in_specs = (
        P(None, "lev", "grp"),
        P(None, ("grp", "lev")),
        P(("grp", "lev")),
        P(("grp", "lev")),
        P(),
    )
    out_specs = (P(), P(None, ("grp", "lev")))
    return jax.shard_map(
        on_device, mesh=mesh, in_specs=in_specs, out_specs=out_specs, check_vma=False
    )
```

```python
import functools

import jax
import jax.numpy as jnp
from jax import lax
from jax.experimental import pallas as pl
from jax.experimental.pallas import tpu as pltpu
from jax.sharding import PartitionSpec as P

MESH = pl.DeviceIdType.MESH
DAYS = 16
MODES = 16
LANES = 128
VMEM_BYTES = 60 * 1024 * 1024
CORES = 2
N_X = 4


def exchange_kernel(
    n_grp, n_lev,
    ocean_ref, clim_hbm, mask_hbm, bottom_hbm, modes_hbm,
    stacked_hbm, gram_ref,
    clim_ref, mask_ref, bottom_ref, modes_ref,
    stacked_ref, recv, clim_rows, limit_rows, weights, anomaly, packed, pair_buf, rs_buf, sum_buf, gather_buf,
    in_sem, local_sem, out_sem, a_send, a_recv, p_sem, r_send, r_recv, s_send, s_recv, g_send, g_recv,
):
    me_g = lax.axis_index("grp")
    me_l = lax.axis_index("lev")
    core = lax.rem(me_g, CORES)
    me_z = me_g // CORES
    n_z = n_grp // CORES
    n_y = n_lev // N_X
    slabs = clim_ref.shape[1] // LANES
    rows = 2 * slabs

    inputs = [
        pltpu.make_async_copy(src, dst, in_sem.at[i])
        for i, (src, dst) in enumerate(
            [(mask_hbm, mask_ref), (bottom_hbm, bottom_ref), (modes_hbm, modes_ref), (clim_hbm, clim_ref)]
        )
    ]
    for copy in inputs:
        copy.start()

    def spiral(i, n):
        half = (i + 1) // 2
        return lax.rem(n // 2 + jnp.where(lax.rem(i, 2) == 1, n - half, half), n)

    def lev_at(o, sign):
        dy, dx = spiral(o // N_X, n_y), spiral(lax.rem(o, N_X), N_X)
        y = lax.rem(me_l // N_X + n_y + sign * dy, n_y)
        x = lax.rem(lax.rem(me_l, N_X) + N_X + sign * dx, N_X)
        return y * N_X + x

    def lev_to(o):
        return lev_at(o, 1)

    def lev_from(o):
        return lev_at(o, -1)

    def z_to(o):
        return lax.rem(me_z + o, n_z)

    def z_from(o):
        return lax.rem(me_z + n_z - o, n_z)

    partner = (me_z * CORES + 1 - core, me_l)

    barrier = pltpu.get_barrier_semaphore()

    @pl.loop(0, n_lev - 1)
    def _(o):
        pl.semaphore_signal(barrier, inc=1, device_id=(me_g, lev_to(o)), device_id_type=MESH)

    @pl.loop(1, n_z)
    def _(o):
        pl.semaphore_signal(
            barrier, inc=1, device_id=(z_to(o) * CORES + core, me_l), device_id_type=MESH
        )

    pl.semaphore_signal(barrier, inc=1, device_id=partner, device_id_type=MESH)
    pl.semaphore_wait(barrier, n_lev + n_z - 1)

    def block_copy(to, slot, k):
        return pltpu.make_async_remote_copy(
            src_ref=ocean_ref.at[:, pl.ds(pl.multiple_of(to * rows, rows), rows), :],
            dst_ref=recv.at[slot],
            send_sem=a_send.at[k],
            recv_sem=a_recv.at[k],
            device_id=(me_g, to),
            device_id_type=MESH,
        )

    @pl.loop(0, n_lev - 1)
    def _(o):
        block_copy(lev_to(o), me_l, o).start()

    own = pltpu.make_async_copy(
        ocean_ref.at[:, pl.ds(pl.multiple_of(me_l * rows, rows), rows), :], recv.at[me_l], local_sem
    )
    own.start()
    for copy in inputs:
        copy.wait()

    limit = jnp.where(mask_ref[...] == 1, bottom_ref[...], 0)
    for slab in range(slabs):
        limit_rows[2 * slab : 2 * slab + 1, :] = limit[slab : slab + 1, :]
        limit_rows[2 * slab + 1 : 2 * slab + 2, :] = limit[slab : slab + 1, :] - 1

    @pl.loop(0, clim_ref.shape[0] // 8)
    def _(t):
        block = clim_ref[pl.ds(pl.multiple_of(t * 8, 8), 8), :]
        for k in range(8):
            for slab in range(slabs):
                row = 2 * slab + k % 2
                clim_rows[4 * t + k // 2, row : row + 1, :] = block[
                    k : k + 1, slab * LANES : (slab + 1) * LANES
                ]

    width = slabs * MODES
    depth = n_lev * rows
    levels = modes_ref.shape[1]
    r = lax.broadcasted_iota(jnp.int32, (width, MODES), 0)
    m = lax.broadcasted_iota(jnp.int32, (width, MODES), 1)
    spread_modes = jnp.where(lax.rem(r, MODES) == m, 1.0, 0.0).astype(jnp.bfloat16)
    l = lax.broadcasted_iota(jnp.int32, (levels, depth), 0)
    q = lax.broadcasted_iota(jnp.int32, (levels, depth), 1)
    spread_levels = jnp.where(2 * (q // rows) + lax.rem(q, 2) == l, 1.0, 0.0).astype(jnp.bfloat16)
    tall = jnp.dot(spread_modes, modes_ref[...], preferred_element_type=jnp.float32).astype(jnp.bfloat16)
    wide = jnp.dot(tall, spread_levels, preferred_element_type=jnp.float32)
    r = lax.broadcasted_iota(jnp.int32, (width, depth), 0)
    q = lax.broadcasted_iota(jnp.int32, (width, depth), 1)
    weights[...] = jnp.where(r // MODES == lax.rem(q, rows) // 2, wide, 0.0).astype(jnp.bfloat16)

    def use(s):
        water = limit_rows[...] > 2 * s
        clim = clim_rows[s]
        for d in range(DAYS):
            diff = recv[s, d].astype(jnp.float32) - clim
            anomaly[pl.ds(pl.multiple_of(s * rows, rows), rows), d * LANES : (d + 1) * LANES] = jnp.where(
                water, diff, 0.0
            ).astype(jnp.bfloat16)

    own.wait()
    use(me_l)

    @pl.loop(0, n_lev - 1)
    def _(o):
        s = lev_from(o)
        block_copy(s, s, o).wait_recv()
        use(s)

    coef = jnp.dot(weights[...], anomaly[...], preferred_element_type=jnp.float32)
    for d in range(DAYS):
        for slab in range(slabs):
            stacked_ref[d * MODES : (d + 1) * MODES, slab * LANES : (slab + 1) * LANES] = coef[
                slab * MODES : (slab + 1) * MODES, d * LANES : (d + 1) * LANES
            ]

    keep = pltpu.make_async_copy(stacked_ref, stacked_hbm, out_sem)
    keep.start()

    half = stacked_ref.shape[0] // 2
    top, low = stacked_ref[:half], stacked_ref[half:]
    long, short = half // n_lev, half // CORES // n_lev

    def gram_block(x, y):
        return lax.dot_general(
            x, y, (((1,), (1,)), ((), ())),
            precision=lax.Precision.HIGHEST, preferred_element_type=jnp.float32,
        )

    last = gram_block(low, low)
    for c, first in enumerate((gram_block(top, top), gram_block(top, low))):
        for i in range(n_lev):
            packed[c, i, :long] = first[i * long : (i + 1) * long]
            at = c * (half // CORES) + i * short
            packed[c, i, long:] = last[at : at + short]

    def pair_copy(src, dst, k):
        return pltpu.make_async_remote_copy(
            src_ref=src, dst_ref=dst, send_sem=p_sem.at[k, 0], recv_sem=p_sem.at[k, 1],
            device_id=partner, device_id_type=MESH,
        )

    to_pair = pair_copy(packed.at[1 - core], pair_buf, 0)
    to_pair.start()
    to_pair.wait()
    packed[core] = packed[core] + pair_buf[...]

    def scatter_copy(to, slot, k):
        return pltpu.make_async_remote_copy(
            src_ref=packed.at[core, to], dst_ref=rs_buf.at[slot],
            send_sem=r_send.at[k], recv_sem=r_recv.at[k],
            device_id=(me_g, to), device_id_type=MESH,
        )

    @pl.loop(0, n_lev - 1)
    def _(o):
        scatter_copy(lev_to(o), me_l, o).start()

    rs_buf[me_l] = packed[core, me_l]

    @pl.loop(0, n_lev - 1)
    def _(o):
        s = lev_from(o)
        scatter_copy(s, s, o).wait_recv()

    sum_buf[me_z] = jnp.sum(rs_buf[...], axis=0)

    def sum_copy(to, slot, k):
        return pltpu.make_async_remote_copy(
            src_ref=sum_buf.at[me_z], dst_ref=sum_buf.at[slot],
            send_sem=s_send.at[k], recv_sem=s_recv.at[k],
            device_id=(to * CORES + core, me_l), device_id_type=MESH,
        )

    @pl.loop(1, n_z)
    def _(o):
        sum_copy(z_to(o), me_z, o).start()

    @pl.loop(1, n_z)
    def _(o):
        s = z_from(o)
        sum_copy(s, s, o).wait_recv()

    total_cols = clim_ref.shape[1] * n_grp * n_lev
    gather_buf[core, me_l] = jnp.sum(sum_buf[...], axis=0) * (1.0 / total_cols)

    def gather_copy(to, slot, k):
        return pltpu.make_async_remote_copy(
            src_ref=gather_buf.at[core, me_l], dst_ref=gather_buf.at[core, slot],
            send_sem=g_send.at[k], recv_sem=g_recv.at[k],
            device_id=(me_g, to), device_id_type=MESH,
        )

    @pl.loop(0, n_lev - 1)
    def _(o):
        gather_copy(lev_to(o), me_l, o).start()

    @pl.loop(0, n_lev - 1)
    def _(o):
        s = lev_from(o)
        gather_copy(s, s, o).wait_recv()

    to_pair = pair_copy(gather_buf.at[core], gather_buf.at[core], 1)
    to_pair.start()
    to_pair.wait()
    for c in range(CORES):
        for i in range(n_lev):
            gram_ref[c, i * long : (i + 1) * long] = gather_buf[c, i, :long]
            at = c * (half // CORES) + i * short
            gram_ref[CORES, at : at + short] = gather_buf[c, i, long:]

    keep.wait()

    @pl.loop(0, n_lev - 1)
    def _(o):
        block_copy(lev_to(o), me_l, o).wait_send()
        scatter_copy(lev_to(o), me_l, o).wait_send()
        gather_copy(lev_to(o), me_l, o).wait_send()

    @pl.loop(1, n_z)
    def _(o):
        sum_copy(z_to(o), me_z, o).wait_send()


def exchange(n_grp, n_lev, ocean, climatology, land_mask, bottom_index, modes):
    days, levels_dev, cols_grp = ocean.shape
    col_dev = climatology.shape[1]
    slabs = col_dev // LANES
    rows = levels_dev * slabs
    width = DAYS * MODES
    half = width // 2
    piece = (half + half // CORES) // n_lev
    tiles = cols_grp // LANES
    ocean = ocean.reshape(days, levels_dev, tiles, LANES).transpose(0, 2, 1, 3)
    ocean = ocean.reshape(days, tiles * levels_dev, LANES)
    vmem = pl.BlockSpec(memory_space=pltpu.VMEM)
    operands = (
        ocean, climatology,
        land_mask.reshape(slabs, LANES), bottom_index.reshape(slabs, LANES), modes,
    )
    return pl.pallas_call(
        functools.partial(exchange_kernel, n_grp, n_lev),
        out_shape=(
            jax.ShapeDtypeStruct((width, col_dev), jnp.float32),
            jax.ShapeDtypeStruct((CORES + 1, half, half), jnp.float32),
        ),
        in_specs=[pl.BlockSpec(memory_space=pltpu.HBM)] * 5,
        out_specs=(pl.BlockSpec(memory_space=pltpu.HBM), vmem),
        scratch_shapes=[
            pltpu.VMEM(climatology.shape, jnp.float32),
            pltpu.VMEM((slabs, LANES), jnp.int32),
            pltpu.VMEM((slabs, LANES), jnp.int32),
            pltpu.VMEM(modes.shape, jnp.bfloat16),
            pltpu.VMEM((width, col_dev), jnp.float32),
            pltpu.VMEM((n_lev, days, rows, LANES), jnp.bfloat16),
            pltpu.VMEM((n_lev, rows, LANES), jnp.float32),
            pltpu.VMEM((rows, LANES), jnp.int32),
            pltpu.VMEM((slabs * MODES, n_lev * rows), jnp.bfloat16),
            pltpu.VMEM((n_lev * rows, days * LANES), jnp.bfloat16),
            pltpu.VMEM((CORES, n_lev, piece, half), jnp.float32),
            pltpu.VMEM((n_lev, piece, half), jnp.float32),
            pltpu.VMEM((n_lev, piece, half), jnp.float32),
            pltpu.VMEM((n_grp // CORES, piece, half), jnp.float32),
            pltpu.VMEM((CORES, n_lev, piece, half), jnp.float32),
            pltpu.SemaphoreType.DMA((4,)),
            pltpu.SemaphoreType.DMA,
            pltpu.SemaphoreType.DMA,
            pltpu.SemaphoreType.DMA((n_lev,)),
            pltpu.SemaphoreType.DMA((n_lev,)),
            pltpu.SemaphoreType.DMA((2, 2)),
            pltpu.SemaphoreType.DMA((n_lev,)),
            pltpu.SemaphoreType.DMA((n_lev,)),
            pltpu.SemaphoreType.DMA((n_grp // CORES,)),
            pltpu.SemaphoreType.DMA((n_grp // CORES,)),
            pltpu.SemaphoreType.DMA((n_lev,)),
            pltpu.SemaphoreType.DMA((n_lev,)),
        ],
        compiler_params=pltpu.CompilerParams(
            collective_id=0, has_side_effects=True, vmem_limit_bytes=VMEM_BYTES
        ),
        name="exchange",
    )(*operands)


def mm(a, b, dims=((1,), (0,))):
    return lax.dot_general(a, b, (dims, ((), ())), precision=lax.Precision.HIGHEST, preferred_element_type=jnp.float32)


def eliminate(a):
    n = a.shape[0]
    w = 8
    lane = lax.broadcasted_iota(jnp.int32, (w, n), 1)
    sub = lax.broadcasted_iota(jnp.int32, (w, n), 0)
    rows = [a[w * h : w * h + w] for h in range(n // w)]

    def spread(x):
        return jnp.broadcast_to(x, (w, n))

    for g in range(n // w):
        at = g * w
        col = [spread(rows[g][:, at + k : at + k + 1]) for k in range(w)]
        row = rows[g]
        pivots, splats = [], []
        for k in range(w):
            inv = 1.0 / spread(col[k][k : k + 1])
            pivot = jnp.where(lane == at + k, inv, spread(row[k : k + 1]) * inv)
            pivots.append(jnp.where((lane > at + k) & (lane < at + w), 0.0, pivot))
            splats.append({j: spread(col[j][k : k + 1]) * inv for j in range(k + 1, w)})
            if k < w - 1:
                m = jnp.where(sub > k, col[k], 0.0)
                row = jnp.where((lane == at + k) & (sub > k), 0.0, row) - m * pivot
                for j in range(k + 1, w):
                    col[j] = col[j] - m * splats[k][j]
        rows[g] = row
        inside = (lane >= at) & (lane < at + w)
        for h in range(g + 1, n // w):
            c = [spread(rows[h][:, at + k : at + k + 1]) for k in range(w)]
            out = jnp.where(inside, 0.0, rows[h])
            for k in range(w):
                for j in range(k + 1, w):
                    c[j] = c[j] - c[k] * splats[k][j]
            for k in range(w):
                out = out - c[k] * pivots[k]
            rows[h] = out
    upper, inverse = [], []
    for h in range(n // w):
        at = sub + w * h
        scale = lax.rsqrt(spread(jnp.sum(jnp.where(lane == at, rows[h], 0.0), axis=1, keepdims=True)))
        upper.append(jnp.where(lane >= at, rows[h] * scale, 0.0))
        inverse.append(jnp.where(lane == at, scale, jnp.where(lane < at, rows[h] * scale, 0.0)))
    return jnp.concatenate(upper, axis=0), jnp.concatenate(inverse, axis=0)

def whiten_kernel(
    gram_hbm, stacked_hbm, factor_hbm, whitened_hbm,
    gram_ref, stacked_ref, factor_ref, whitened_ref, sem,
):
    half = gram_ref.shape[1]
    gram_in = pltpu.make_async_copy(gram_hbm, gram_ref, sem.at[0])
    stacked_in = pltpu.make_async_copy(stacked_hbm, stacked_ref, sem.at[1])
    first_out = pltpu.make_async_copy(whitened_ref.at[:half], whitened_hbm.at[:half], sem.at[2])
    second_out = pltpu.make_async_copy(whitened_ref.at[half:], whitened_hbm.at[half:], sem.at[3])
    factor_out = pltpu.make_async_copy(factor_ref, factor_hbm, sem.at[4])
    gram_in.start()
    stacked_in.start()
    gram_in.wait()
    r11, i11 = eliminate(gram_ref[0])
    r12 = mm(i11, gram_ref[1])
    factor_ref[:half, :half] = r11
    factor_ref[:half, half:] = r12
    factor_ref[half:, :half] = jnp.zeros((half, half), jnp.float32)
    rest = gram_ref[2] - mm(r12, r12, ((0,), (0,)))
    stacked_in.wait()
    first = mm(i11, stacked_ref[:half])
    whitened_ref[:half] = first
    first_out.start()
    left = stacked_ref[half:] - mm(r12, first, ((0,), (0,)))
    r22, i22 = eliminate(rest)
    factor_ref[half:, half:] = r22
    factor_out.start()
    whitened_ref[half:] = mm(i22, left)
    second_out.start()
    first_out.wait()
    factor_out.wait()
    second_out.wait()


def whiten(gram, stacked):
    hbm = pl.BlockSpec(memory_space=pltpu.HBM)
    factor_shape = (stacked.shape[0],) * 2
    return pl.pallas_call(
        whiten_kernel,
        out_shape=(
            jax.ShapeDtypeStruct(factor_shape, jnp.float32),
            jax.ShapeDtypeStruct(stacked.shape, jnp.float32),
        ),
        in_specs=[hbm, hbm],
        out_specs=(hbm, hbm),
        scratch_shapes=[
            pltpu.VMEM(gram.shape, jnp.float32),
            pltpu.VMEM(stacked.shape, jnp.float32),
            pltpu.VMEM(factor_shape, jnp.float32),
            pltpu.VMEM(stacked.shape, jnp.float32),
            pltpu.SemaphoreType.DMA((5,)),
        ],
        compiler_params=pltpu.CompilerParams(vmem_limit_bytes=VMEM_BYTES),
        name="whiten",
    )(gram, stacked)


def solution(mesh):
    n_grp, n_lev = mesh.shape["grp"], mesh.shape["lev"]

    def on_device(ocean_field, climatology, land_mask, bottom_index, vertical_modes):
        stacked, gram = exchange(
            n_grp, n_lev, ocean_field, climatology, land_mask, bottom_index, vertical_modes
        )
        return whiten(gram, stacked)

    in_specs = (
        P(None, "lev", "grp"),
        P(None, ("grp", "lev")),
        P(("grp", "lev")),
        P(("grp", "lev")),
        P(),
    )
    out_specs = (P(), P(None, ("grp", "lev")))
    return jax.shard_map(
        on_device, mesh=mesh, in_specs=in_specs, out_specs=out_specs, check_vma=False
    )
```

```python
import functools

import jax
import jax.numpy as jnp
from jax import lax
from jax.experimental import pallas as pl
from jax.experimental.pallas import tpu as pltpu
from jax.sharding import PartitionSpec as P

MESH = pl.DeviceIdType.MESH
DAYS = 16
MODES = 16
LANES = 128
VMEM_BYTES = 60 * 1024 * 1024
CORES = 2
N_X = 4


def exchange_kernel(
    n_grp, n_lev,
    ocean_ref, clim_hbm, mask_hbm, bottom_hbm, modes_hbm,
    stacked_hbm, gram_hbm,
    clim_ref, mask_ref, bottom_ref, modes_ref,
    stacked_ref, recv, clim_rows, limit_rows, weights, anomaly, theirs, packed, pair_buf, rs_buf, sum_buf, gather_buf,
    in_sem, local_sem, out_sem, a_send, a_recv, p_sem, r_send, r_recv, s_send, s_recv, g_send, g_recv,
):
    me_g = lax.axis_index("grp")
    me_l = lax.axis_index("lev")
    core = lax.rem(me_g, CORES)
    me_z = me_g // CORES
    n_z = n_grp // CORES
    n_y = n_lev // N_X
    slabs = clim_ref.shape[1] // LANES
    rows = 2 * slabs

    inputs = [
        pltpu.make_async_copy(src, dst, in_sem.at[i])
        for i, (src, dst) in enumerate(
            [(mask_hbm, mask_ref), (bottom_hbm, bottom_ref), (modes_hbm, modes_ref), (clim_hbm, clim_ref)]
        )
    ]
    for copy in inputs:
        copy.start()

    def far_first(n):
        return sorted(range(n), key=lambda d: -min(d, n - d))

    y_at = [lax.rem(me_l // N_X + d, n_y) * N_X for d in range(n_y)]
    x_at = [lax.rem(lax.rem(me_l, N_X) + d, N_X) for d in range(N_X)]
    steps = [(dy, dx) for dy in far_first(n_y) for dx in far_first(N_X)][:-1]
    peers = [y_at[dy] + x_at[dx] for dy, dx in steps]
    senders = [y_at[-dy % n_y] + x_at[-dx % N_X] for dy, dx in steps]

    def spiral(i, n):
        half = (i + 1) // 2
        return lax.rem(n // 2 + jnp.where(lax.rem(i, 2) == 1, half, n - half), n)

    def sender(o):
        y = lax.rem(me_l // N_X + spiral(o // N_X, n_y), n_y)
        x = lax.rem(lax.rem(me_l, N_X) + spiral(lax.rem(o, N_X), N_X), N_X)
        return y * N_X + x

    def z_to(o):
        return lax.rem(me_z + o, n_z)

    def z_from(o):
        return lax.rem(me_z + n_z - o, n_z)

    partner = (me_z * CORES + 1 - core, me_l)

    barrier = pltpu.get_barrier_semaphore()

    for peer in peers:
        pl.semaphore_signal(barrier, inc=1, device_id=(me_g, peer), device_id_type=MESH)
    for o in range(1, n_z):
        pl.semaphore_signal(
            barrier, inc=1, device_id=(z_to(o) * CORES + core, me_l), device_id_type=MESH
        )

    pl.semaphore_signal(barrier, inc=1, device_id=partner, device_id_type=MESH)
    pl.semaphore_wait(barrier, n_lev + n_z - 1)

    def block_copy(to, slot, k):
        return pltpu.make_async_remote_copy(
            src_ref=ocean_ref.at[:, pl.ds(pl.multiple_of(to * rows, rows), rows), :],
            dst_ref=recv.at[slot],
            send_sem=a_send.at[k],
            recv_sem=a_recv.at[k],
            device_id=(me_g, to),
            device_id_type=MESH,
        )

    for o, peer in enumerate(peers):
        block_copy(peer, me_l, o).start()

    own = pltpu.make_async_copy(
        ocean_ref.at[:, pl.ds(pl.multiple_of(me_l * rows, rows), rows), :], recv.at[me_l], local_sem
    )
    own.start()
    for copy in inputs:
        copy.wait()

    limit = jnp.where(mask_ref[...] == 1, bottom_ref[...], 0)
    for slab in range(slabs):
        limit_rows[2 * slab : 2 * slab + 1, :] = limit[slab : slab + 1, :]
        limit_rows[2 * slab + 1 : 2 * slab + 2, :] = limit[slab : slab + 1, :] - 1

    @pl.loop(0, clim_ref.shape[0] // 8)
    def _(t):
        block = clim_ref[pl.ds(pl.multiple_of(t * 8, 8), 8), :]
        for k in range(8):
            for slab in range(slabs):
                row = 2 * slab + k % 2
                clim_rows[4 * t + k // 2, row : row + 1, :] = block[
                    k : k + 1, slab * LANES : (slab + 1) * LANES
                ]

    width = slabs * MODES
    depth = n_lev * rows
    levels = modes_ref.shape[1]
    r = lax.broadcasted_iota(jnp.int32, (width, MODES), 0)
    m = lax.broadcasted_iota(jnp.int32, (width, MODES), 1)
    spread_modes = jnp.where(lax.rem(r, MODES) == m, 1.0, 0.0).astype(jnp.bfloat16)
    l = lax.broadcasted_iota(jnp.int32, (levels, depth), 0)
    q = lax.broadcasted_iota(jnp.int32, (levels, depth), 1)
    spread_levels = jnp.where(2 * (q // rows) + lax.rem(q, 2) == l, 1.0, 0.0).astype(jnp.bfloat16)
    tall = jnp.dot(spread_modes, modes_ref[...], preferred_element_type=jnp.float32).astype(jnp.bfloat16)
    wide = jnp.dot(tall, spread_levels, preferred_element_type=jnp.float32)
    r = lax.broadcasted_iota(jnp.int32, (width, depth), 0)
    q = lax.broadcasted_iota(jnp.int32, (width, depth), 1)
    weights[...] = jnp.where(r // MODES == lax.rem(q, rows) // 2, wide, 0.0).astype(jnp.bfloat16)

    def use(s):
        water = limit_rows[...] > 2 * s
        clim = clim_rows[s]
        for d in range(DAYS):
            diff = recv[s, d].astype(jnp.float32) - clim
            anomaly[pl.ds(pl.multiple_of(s * rows, rows), rows), d * LANES : (d + 1) * LANES] = jnp.where(
                water, diff, 0.0
            ).astype(jnp.bfloat16)

    own.wait()
    use(me_l)

    @pl.loop(0, n_lev - 1)
    def _(o):
        s = sender(o)
        block_copy(s, s, o).wait_recv()
        use(s)

    coef = jnp.dot(weights[...], anomaly[...], preferred_element_type=jnp.float32)
    for d in range(DAYS):
        for slab in range(slabs):
            stacked_ref[d * MODES : (d + 1) * MODES, slab * LANES : (slab + 1) * LANES] = coef[
                slab * MODES : (slab + 1) * MODES, d * LANES : (d + 1) * LANES
            ]

    keep = pltpu.make_async_copy(stacked_ref, stacked_hbm, out_sem.at[0])
    keep.start()

    half = stacked_ref.shape[0] // 2
    share = half // CORES
    long, short = half // n_lev, share // n_lev

    def gram_block(x, y):
        return lax.dot_general(
            x, y, (((1,), (1,)), ((), ())),
            precision=lax.Precision.HIGHEST, preferred_element_type=jnp.float32,
        )

    def pack(c, out):
        row, rest = pl.multiple_of(c * half, half), pl.multiple_of(half + c * share, share)
        first = gram_block(stacked_ref[:half], stacked_ref[pl.ds(row, half)])
        last = gram_block(stacked_ref[pl.ds(rest, share)], stacked_ref[half:])
        for i in range(n_lev):
            out[i, :long] = first[i * long : (i + 1) * long]
            out[i, long:] = last[i * short : (i + 1) * short]

    def pair_copy(src, dst, k):
        return pltpu.make_async_remote_copy(
            src_ref=src, dst_ref=dst, send_sem=p_sem.at[k, 0], recv_sem=p_sem.at[k, 1],
            device_id=partner, device_id_type=MESH,
        )

    pack(1 - core, theirs)
    to_pair = pair_copy(theirs, pair_buf, 0)
    to_pair.start()
    pack(core, packed)
    to_pair.wait()
    packed[...] = packed[...] + pair_buf[...]

    def scatter_copy(to, slot, k):
        return pltpu.make_async_remote_copy(
            src_ref=packed.at[to], dst_ref=rs_buf.at[slot],
            send_sem=r_send.at[k], recv_sem=r_recv.at[k],
            device_id=(me_g, to), device_id_type=MESH,
        )

    for o, peer in enumerate(peers):
        scatter_copy(peer, me_l, o).start()

    rs_buf[me_l] = packed[me_l]

    for o, s in enumerate(senders):
        scatter_copy(s, s, o).wait_recv()

    sum_buf[me_z] = jnp.sum(rs_buf[...], axis=0)

    def sum_copy(to, slot, k):
        return pltpu.make_async_remote_copy(
            src_ref=sum_buf.at[me_z], dst_ref=sum_buf.at[slot],
            send_sem=s_send.at[k], recv_sem=s_recv.at[k],
            device_id=(to * CORES + core, me_l), device_id_type=MESH,
        )

    for o in range(1, n_z):
        sum_copy(z_to(o), me_z, o).start()
    for o in range(1, n_z):
        s = z_from(o)
        sum_copy(s, s, o).wait_recv()

    total_cols = clim_ref.shape[1] * n_grp * n_lev
    gather_buf[core, me_l] = jnp.sum(sum_buf[...], axis=0) * (1.0 / total_cols)

    def gather_copy(to, slot, k):
        return pltpu.make_async_remote_copy(
            src_ref=gather_buf.at[core, me_l], dst_ref=gather_buf.at[core, slot],
            send_sem=g_send.at[k], recv_sem=g_recv.at[k],
            device_id=(me_g, to), device_id_type=MESH,
        )

    for o, peer in enumerate(peers):
        gather_copy(peer, me_l, o).start()
    for o, s in enumerate(senders):
        gather_copy(s, s, o).wait_recv()

    to_pair = pair_copy(gather_buf.at[core], gather_buf.at[core], 1)
    to_pair.start()
    mine = pltpu.make_async_copy(gather_buf.at[core], gram_hbm.at[core], out_sem.at[1])
    mine.start()
    to_pair.wait()
    other = pltpu.make_async_copy(gather_buf.at[1 - core], gram_hbm.at[1 - core], out_sem.at[2])
    other.start()
    for o, peer in enumerate(peers):
        block_copy(peer, me_l, o).wait_send()
        scatter_copy(peer, me_l, o).wait_send()
        gather_copy(peer, me_l, o).wait_send()
    for o in range(1, n_z):
        sum_copy(z_to(o), me_z, o).wait_send()
    keep.wait()
    mine.wait()
    other.wait()


def exchange(n_grp, n_lev, ocean, climatology, land_mask, bottom_index, modes):
    days, levels_dev, cols_grp = ocean.shape
    col_dev = climatology.shape[1]
    slabs = col_dev // LANES
    rows = levels_dev * slabs
    width = DAYS * MODES
    half = width // 2
    piece = (half + half // CORES) // n_lev
    tiles = cols_grp // LANES
    ocean = ocean.reshape(days, levels_dev, tiles, LANES).transpose(0, 2, 1, 3)
    ocean = ocean.reshape(days, tiles * levels_dev, LANES)
    hbm = pl.BlockSpec(memory_space=pltpu.HBM)
    operands = (
        ocean, climatology,
        land_mask.reshape(slabs, LANES), bottom_index.reshape(slabs, LANES), modes,
    )
    return pl.pallas_call(
        functools.partial(exchange_kernel, n_grp, n_lev),
        out_shape=(
            jax.ShapeDtypeStruct((width, col_dev), jnp.float32),
            jax.ShapeDtypeStruct((CORES, n_lev, piece, half), jnp.float32),
        ),
        in_specs=[hbm] * 5,
        out_specs=(hbm, hbm),
        scratch_shapes=[
            pltpu.VMEM(climatology.shape, jnp.float32),
            pltpu.VMEM((slabs, LANES), jnp.int32),
            pltpu.VMEM((slabs, LANES), jnp.int32),
            pltpu.VMEM(modes.shape, jnp.bfloat16),
            pltpu.VMEM((width, col_dev), jnp.float32),
            pltpu.VMEM((n_lev, days, rows, LANES), jnp.bfloat16),
            pltpu.VMEM((n_lev, rows, LANES), jnp.float32),
            pltpu.VMEM((rows, LANES), jnp.int32),
            pltpu.VMEM((slabs * MODES, n_lev * rows), jnp.bfloat16),
            pltpu.VMEM((n_lev * rows, days * LANES), jnp.bfloat16),
            pltpu.VMEM((n_lev, piece, half), jnp.float32),
            pltpu.VMEM((n_lev, piece, half), jnp.float32),
            pltpu.VMEM((n_lev, piece, half), jnp.float32),
            pltpu.VMEM((n_lev, piece, half), jnp.float32),
            pltpu.VMEM((n_grp // CORES, piece, half), jnp.float32),
            pltpu.VMEM((CORES, n_lev, piece, half), jnp.float32),
            pltpu.SemaphoreType.DMA((4,)),
            pltpu.SemaphoreType.DMA,
            pltpu.SemaphoreType.DMA((3,)),
            pltpu.SemaphoreType.DMA((n_lev,)),
            pltpu.SemaphoreType.DMA((n_lev,)),
            pltpu.SemaphoreType.DMA((2, 2)),
            pltpu.SemaphoreType.DMA((n_lev,)),
            pltpu.SemaphoreType.DMA((n_lev,)),
            pltpu.SemaphoreType.DMA((n_grp // CORES,)),
            pltpu.SemaphoreType.DMA((n_grp // CORES,)),
            pltpu.SemaphoreType.DMA((n_lev,)),
            pltpu.SemaphoreType.DMA((n_lev,)),
        ],
        compiler_params=pltpu.CompilerParams(
            collective_id=0, has_side_effects=True, vmem_limit_bytes=VMEM_BYTES
        ),
        name="exchange",
    )(*operands)


def mm(a, b, dims=((1,), (0,))):
    return lax.dot_general(a, b, (dims, ((), ())), precision=lax.Precision.HIGHEST, preferred_element_type=jnp.float32)


def eliminate(a):
    n = a.shape[0]
    w = 8
    lane = lax.broadcasted_iota(jnp.int32, (w, n), 1)
    sub = lax.broadcasted_iota(jnp.int32, (w, n), 0)
    rows = [a[w * h : w * h + w] for h in range(n // w)]

    def spread(x):
        return jnp.broadcast_to(x, (w, n))

    for g in range(n // w):
        at = g * w
        col = [spread(rows[g][:, at + k : at + k + 1]) for k in range(w)]
        row = rows[g]
        pivots, splats = [], []
        for k in range(w):
            inv = 1.0 / spread(col[k][k : k + 1])
            pivot = jnp.where(lane == at + k, inv, spread(row[k : k + 1]) * inv)
            pivots.append(jnp.where((lane > at + k) & (lane < at + w), 0.0, pivot))
            splats.append({j: spread(col[j][k : k + 1]) * inv for j in range(k + 1, w)})
            if k < w - 1:
                m = jnp.where(sub > k, col[k], 0.0)
                row = jnp.where((lane == at + k) & (sub > k), 0.0, row) - m * pivot
                for j in range(k + 1, w):
                    col[j] = col[j] - m * splats[k][j]
        rows[g] = row
        inside = (lane >= at) & (lane < at + w)
        for h in range(g + 1, n // w):
            c = [spread(rows[h][:, at + k : at + k + 1]) for k in range(w)]
            out = jnp.where(inside, 0.0, rows[h])
            for k in range(w):
                for j in range(k + 1, w):
                    c[j] = c[j] - c[k] * splats[k][j]
            for k in range(w):
                out = out - c[k] * pivots[k]
            rows[h] = out
    upper, inverse = [], []
    for h in range(n // w):
        at = sub + w * h
        scale = lax.rsqrt(spread(jnp.sum(jnp.where(lane == at, rows[h], 0.0), axis=1, keepdims=True)))
        upper.append(jnp.where(lane >= at, rows[h] * scale, 0.0))
        inverse.append(jnp.where(lane == at, scale, jnp.where(lane < at, rows[h] * scale, 0.0)))
    return jnp.concatenate(upper, axis=0), jnp.concatenate(inverse, axis=0)

def whiten_kernel(
    gram_hbm, stacked_hbm, factor_hbm, whitened_hbm,
    pieces, gram_ref, stacked_ref, factor_ref, whitened_ref, sem,
):
    half = gram_ref.shape[1]
    long, short = half // pieces.shape[1], half // CORES // pieces.shape[1]
    gram_in = pltpu.make_async_copy(gram_hbm, pieces, sem.at[0])
    stacked_in = pltpu.make_async_copy(stacked_hbm, stacked_ref, sem.at[1])
    first_out = pltpu.make_async_copy(whitened_ref.at[:half], whitened_hbm.at[:half], sem.at[2])
    second_out = pltpu.make_async_copy(whitened_ref.at[half:], whitened_hbm.at[half:], sem.at[3])
    factor_out = pltpu.make_async_copy(factor_ref, factor_hbm, sem.at[4])
    gram_in.start()
    stacked_in.start()
    gram_in.wait()
    for c in range(CORES):
        for i in range(pieces.shape[1]):
            gram_ref[c, i * long : (i + 1) * long] = pieces[c, i, :long]
            at = c * (half // CORES) + i * short
            gram_ref[CORES, at : at + short] = pieces[c, i, long:]
    r11, i11 = eliminate(gram_ref[0])
    r12 = mm(i11, gram_ref[1])
    factor_ref[:half, :half] = r11
    factor_ref[:half, half:] = r12
    factor_ref[half:, :half] = jnp.zeros((half, half), jnp.float32)
    rest = gram_ref[2] - mm(r12, r12, ((0,), (0,)))
    stacked_in.wait()
    first = mm(i11, stacked_ref[:half])
    whitened_ref[:half] = first
    first_out.start()
    left = stacked_ref[half:] - mm(r12, first, ((0,), (0,)))
    r22, i22 = eliminate(rest)
    factor_ref[half:, half:] = r22
    factor_out.start()
    whitened_ref[half:] = mm(i22, left)
    second_out.start()
    first_out.wait()
    factor_out.wait()
    second_out.wait()


def whiten(gram, stacked):
    hbm = pl.BlockSpec(memory_space=pltpu.HBM)
    factor_shape = (stacked.shape[0],) * 2
    return pl.pallas_call(
        whiten_kernel,
        out_shape=(
            jax.ShapeDtypeStruct(factor_shape, jnp.float32),
            jax.ShapeDtypeStruct(stacked.shape, jnp.float32),
        ),
        in_specs=[hbm, hbm],
        out_specs=(hbm, hbm),
        scratch_shapes=[
            pltpu.VMEM(gram.shape, jnp.float32),
            pltpu.VMEM((CORES + 1, gram.shape[3], gram.shape[3]), jnp.float32),
            pltpu.VMEM(stacked.shape, jnp.float32),
            pltpu.VMEM(factor_shape, jnp.float32),
            pltpu.VMEM(stacked.shape, jnp.float32),
            pltpu.SemaphoreType.DMA((5,)),
        ],
        compiler_params=pltpu.CompilerParams(vmem_limit_bytes=VMEM_BYTES),
        name="whiten",
    )(gram, stacked)


def solution(mesh):
    n_grp, n_lev = mesh.shape["grp"], mesh.shape["lev"]

    def on_device(ocean_field, climatology, land_mask, bottom_index, vertical_modes):
        stacked, gram = exchange(
            n_grp, n_lev, ocean_field, climatology, land_mask, bottom_index, vertical_modes
        )
        return whiten(gram, stacked)

    in_specs = (
        P(None, "lev", "grp"),
        P(None, ("grp", "lev")),
        P(("grp", "lev")),
        P(("grp", "lev")),
        P(),
    )
    out_specs = (P(), P(None, ("grp", "lev")))
    return jax.shard_map(
        on_device, mesh=mesh, in_specs=in_specs, out_specs=out_specs, check_vma=False
    )
```

```python
import functools

import jax
import jax.numpy as jnp
from jax import lax
from jax.experimental import pallas as pl
from jax.experimental.pallas import tpu as pltpu
from jax.sharding import PartitionSpec as P

MESH = pl.DeviceIdType.MESH
DAYS = 16
MODES = 16
LANES = 128
VMEM_BYTES = 40 * 1024 * 1024
CORES = 2
N_X = 4


def exchange_kernel(
    n_grp, n_lev,
    ocean_ref, clim_hbm, mask_hbm, bottom_hbm, modes_hbm,
    stacked_ref, gram_ref,
    clim_ref, mask_ref, bottom_ref, modes_ref,
    recv, clim_rows, limit_rows, weights, anomaly, theirs, packed, pair_buf, rs_buf, sum_buf, gather_buf,
    in_sem, local_sem, a_send, a_recv, p_sem, r_send, r_recv, s_send, s_recv, g_send, g_recv,
):
    me_g = lax.axis_index("grp")
    me_l = lax.axis_index("lev")
    core = lax.rem(me_g, CORES)
    me_z = me_g // CORES
    n_z = n_grp // CORES
    n_y = n_lev // N_X
    slabs = clim_ref.shape[1] // LANES
    rows = 2 * slabs

    inputs = [
        pltpu.make_async_copy(src, dst, in_sem.at[i])
        for i, (src, dst) in enumerate(
            [(mask_hbm, mask_ref), (bottom_hbm, bottom_ref), (modes_hbm, modes_ref), (clim_hbm, clim_ref)]
        )
    ]
    for copy in inputs:
        copy.start()

    def far_first(n):
        return sorted(range(n), key=lambda d: -min(d, n - d))

    y_at = [lax.rem(me_l // N_X + d, n_y) * N_X for d in range(n_y)]
    x_at = [lax.rem(lax.rem(me_l, N_X) + d, N_X) for d in range(N_X)]
    steps = [(dy, dx) for dy in far_first(n_y) for dx in far_first(N_X)][:-1]
    peers = [y_at[dy] + x_at[dx] for dy, dx in steps]
    senders = [y_at[-dy % n_y] + x_at[-dx % N_X] for dy, dx in steps]

    def spiral(i, n):
        half = (i + 1) // 2
        return lax.rem(n // 2 + jnp.where(lax.rem(i, 2) == 1, half, n - half), n)

    def sender(o):
        y = lax.rem(me_l // N_X + spiral(o // N_X, n_y), n_y)
        x = lax.rem(lax.rem(me_l, N_X) + spiral(lax.rem(o, N_X), N_X), N_X)
        return y * N_X + x

    def z_to(o):
        return lax.rem(me_z + o, n_z)

    def z_from(o):
        return lax.rem(me_z + n_z - o, n_z)

    partner = (me_z * CORES + 1 - core, me_l)

    barrier = pltpu.get_barrier_semaphore()

    for peer in peers:
        pl.semaphore_signal(barrier, inc=1, device_id=(me_g, peer), device_id_type=MESH)
    for o in range(1, n_z):
        pl.semaphore_signal(
            barrier, inc=1, device_id=(z_to(o) * CORES + core, me_l), device_id_type=MESH
        )

    pl.semaphore_signal(barrier, inc=1, device_id=partner, device_id_type=MESH)
    pl.semaphore_wait(barrier, n_lev + n_z - 1)

    def block_copy(to, slot, k):
        return pltpu.make_async_remote_copy(
            src_ref=ocean_ref.at[:, pl.ds(pl.multiple_of(to * rows, rows), rows), :],
            dst_ref=recv.at[slot],
            send_sem=a_send.at[k],
            recv_sem=a_recv.at[k],
            device_id=(me_g, to),
            device_id_type=MESH,
        )

    for o, peer in enumerate(peers):
        block_copy(peer, me_l, o).start()

    own = pltpu.make_async_copy(
        ocean_ref.at[:, pl.ds(pl.multiple_of(me_l * rows, rows), rows), :], recv.at[me_l], local_sem
    )
    own.start()
    for copy in inputs:
        copy.wait()

    limit = jnp.where(mask_ref[...] == 1, bottom_ref[...], 0)
    for slab in range(slabs):
        limit_rows[2 * slab : 2 * slab + 1, :] = limit[slab : slab + 1, :]
        limit_rows[2 * slab + 1 : 2 * slab + 2, :] = limit[slab : slab + 1, :] - 1

    @pl.loop(0, clim_ref.shape[0] // 8)
    def _(t):
        block = clim_ref[pl.ds(pl.multiple_of(t * 8, 8), 8), :]
        for k in range(8):
            for slab in range(slabs):
                row = 2 * slab + k % 2
                clim_rows[4 * t + k // 2, row : row + 1, :] = block[
                    k : k + 1, slab * LANES : (slab + 1) * LANES
                ]

    width = slabs * MODES
    depth = n_lev * rows
    levels = modes_ref.shape[1]
    r = lax.broadcasted_iota(jnp.int32, (width, MODES), 0)
    m = lax.broadcasted_iota(jnp.int32, (width, MODES), 1)
    spread_modes = jnp.where(lax.rem(r, MODES) == m, 1.0, 0.0).astype(jnp.bfloat16)
    l = lax.broadcasted_iota(jnp.int32, (levels, depth), 0)
    q = lax.broadcasted_iota(jnp.int32, (levels, depth), 1)
    spread_levels = jnp.where(2 * (q // rows) + lax.rem(q, 2) == l, 1.0, 0.0).astype(jnp.bfloat16)
    tall = jnp.dot(spread_modes, modes_ref[...], preferred_element_type=jnp.float32).astype(jnp.bfloat16)
    wide = jnp.dot(tall, spread_levels, preferred_element_type=jnp.float32)
    r = lax.broadcasted_iota(jnp.int32, (width, depth), 0)
    q = lax.broadcasted_iota(jnp.int32, (width, depth), 1)
    weights[...] = jnp.where(r // MODES == lax.rem(q, rows) // 2, wide, 0.0).astype(jnp.bfloat16)

    def use(s):
        water = limit_rows[...] > 2 * s
        clim = clim_rows[s]
        for d in range(DAYS):
            diff = recv[s, d].astype(jnp.float32) - clim
            anomaly[pl.ds(pl.multiple_of(s * rows, rows), rows), d * LANES : (d + 1) * LANES] = jnp.where(
                water, diff, 0.0
            ).astype(jnp.bfloat16)

    own.wait()
    use(me_l)

    @pl.loop(0, n_lev - 1)
    def _(o):
        s = sender(o)
        block_copy(s, s, o).wait_recv()
        use(s)

    coef = jnp.dot(weights[...], anomaly[...], preferred_element_type=jnp.float32)
    for d in range(DAYS):
        for slab in range(slabs):
            stacked_ref[d * MODES : (d + 1) * MODES, slab * LANES : (slab + 1) * LANES] = coef[
                slab * MODES : (slab + 1) * MODES, d * LANES : (d + 1) * LANES
            ]

    half = stacked_ref.shape[0] // 2
    share = half // CORES
    long, short = half // n_lev, share // n_lev

    def gram_block(x, y):
        return lax.dot_general(
            x, y, (((1,), (1,)), ((), ())),
            precision=lax.Precision.HIGHEST, preferred_element_type=jnp.float32,
        )

    def pack(c, out):
        row, rest = pl.multiple_of(c * half, half), pl.multiple_of(half + c * share, share)
        first = gram_block(stacked_ref[:half], stacked_ref[pl.ds(row, half)])
        last = gram_block(stacked_ref[pl.ds(rest, share)], stacked_ref[half:])
        for i in range(n_lev):
            out[i, :long] = first[i * long : (i + 1) * long]
            out[i, long:] = last[i * short : (i + 1) * short]

    def pair_copy(src, dst, k):
        return pltpu.make_async_remote_copy(
            src_ref=src, dst_ref=dst, send_sem=p_sem.at[k, 0], recv_sem=p_sem.at[k, 1],
            device_id=partner, device_id_type=MESH,
        )

    pack(1 - core, theirs)
    to_pair = pair_copy(theirs, pair_buf, 0)
    to_pair.start()
    pack(core, packed)
    to_pair.wait()
    packed[...] = packed[...] + pair_buf[...]

    def scatter_copy(to, slot, k):
        return pltpu.make_async_remote_copy(
            src_ref=packed.at[to], dst_ref=rs_buf.at[slot],
            send_sem=r_send.at[k], recv_sem=r_recv.at[k],
            device_id=(me_g, to), device_id_type=MESH,
        )

    for o, peer in enumerate(peers):
        scatter_copy(peer, me_l, o).start()

    rs_buf[me_l] = packed[me_l]

    for o, s in enumerate(senders):
        scatter_copy(s, s, o).wait_recv()

    sum_buf[me_z] = jnp.sum(rs_buf[...], axis=0)

    def sum_copy(to, slot, k):
        return pltpu.make_async_remote_copy(
            src_ref=sum_buf.at[me_z], dst_ref=sum_buf.at[slot],
            send_sem=s_send.at[k], recv_sem=s_recv.at[k],
            device_id=(to * CORES + core, me_l), device_id_type=MESH,
        )

    for o in range(1, n_z):
        sum_copy(z_to(o), me_z, o).start()
    for o in range(1, n_z):
        s = z_from(o)
        sum_copy(s, s, o).wait_recv()

    total_cols = clim_ref.shape[1] * n_grp * n_lev
    gather_buf[core, me_l] = jnp.sum(sum_buf[...], axis=0) * (1.0 / total_cols)

    def gather_copy(to, slot, k):
        return pltpu.make_async_remote_copy(
            src_ref=gather_buf.at[core, me_l], dst_ref=gather_buf.at[core, slot],
            send_sem=g_send.at[k], recv_sem=g_recv.at[k],
            device_id=(me_g, to), device_id_type=MESH,
        )

    for o, peer in enumerate(peers):
        gather_copy(peer, me_l, o).start()
    for o, s in enumerate(senders):
        gather_copy(s, s, o).wait_recv()

    to_pair = pair_copy(gather_buf.at[core], gather_buf.at[core], 1)
    to_pair.start()
    gram_ref[core] = gather_buf[core]
    to_pair.wait()
    gram_ref[1 - core] = gather_buf[1 - core]
    for o, peer in enumerate(peers):
        block_copy(peer, me_l, o).wait_send()
        scatter_copy(peer, me_l, o).wait_send()
        gather_copy(peer, me_l, o).wait_send()
    for o in range(1, n_z):
        sum_copy(z_to(o), me_z, o).wait_send()


def exchange(n_grp, n_lev, ocean, climatology, land_mask, bottom_index, modes):
    days, levels_dev, cols_grp = ocean.shape
    col_dev = climatology.shape[1]
    slabs = col_dev // LANES
    rows = levels_dev * slabs
    width = DAYS * MODES
    half = width // 2
    piece = (half + half // CORES) // n_lev
    tiles = cols_grp // LANES
    ocean = ocean.reshape(days, levels_dev, tiles, LANES).transpose(0, 2, 1, 3)
    ocean = ocean.reshape(days, tiles * levels_dev, LANES)
    vmem, hbm = pl.BlockSpec(memory_space=pltpu.VMEM), pl.BlockSpec(memory_space=pltpu.HBM)
    operands = (
        ocean, climatology,
        land_mask.reshape(slabs, LANES), bottom_index.reshape(slabs, LANES), modes,
    )
    operands = [pltpu.with_memory_space_constraint(x, pltpu.HBM) for x in operands]
    return pl.pallas_call(
        functools.partial(exchange_kernel, n_grp, n_lev),
        out_shape=(
            jax.ShapeDtypeStruct((width, col_dev), jnp.float32),
            jax.ShapeDtypeStruct((CORES, n_lev, piece, half), jnp.float32),
        ),
        in_specs=[hbm] * 5,
        out_specs=(vmem, vmem),
        scratch_shapes=[
            pltpu.VMEM(climatology.shape, jnp.float32),
            pltpu.VMEM((slabs, LANES), jnp.int32),
            pltpu.VMEM((slabs, LANES), jnp.int32),
            pltpu.VMEM(modes.shape, jnp.bfloat16),
            pltpu.VMEM((n_lev, days, rows, LANES), jnp.bfloat16),
            pltpu.VMEM((n_lev, rows, LANES), jnp.float32),
            pltpu.VMEM((rows, LANES), jnp.int32),
            pltpu.VMEM((slabs * MODES, n_lev * rows), jnp.bfloat16),
            pltpu.VMEM((n_lev * rows, days * LANES), jnp.bfloat16),
            pltpu.VMEM((n_lev, piece, half), jnp.float32),
            pltpu.VMEM((n_lev, piece, half), jnp.float32),
            pltpu.VMEM((n_lev, piece, half), jnp.float32),
            pltpu.VMEM((n_lev, piece, half), jnp.float32),
            pltpu.VMEM((n_grp // CORES, piece, half), jnp.float32),
            pltpu.VMEM((CORES, n_lev, piece, half), jnp.float32),
            pltpu.SemaphoreType.DMA((4,)),
            pltpu.SemaphoreType.DMA,
            pltpu.SemaphoreType.DMA((n_lev,)),
            pltpu.SemaphoreType.DMA((n_lev,)),
            pltpu.SemaphoreType.DMA((2, 2)),
            pltpu.SemaphoreType.DMA((n_lev,)),
            pltpu.SemaphoreType.DMA((n_lev,)),
            pltpu.SemaphoreType.DMA((n_grp // CORES,)),
            pltpu.SemaphoreType.DMA((n_grp // CORES,)),
            pltpu.SemaphoreType.DMA((n_lev,)),
            pltpu.SemaphoreType.DMA((n_lev,)),
        ],
        compiler_params=pltpu.CompilerParams(
            collective_id=0, has_side_effects=True, vmem_limit_bytes=VMEM_BYTES
        ),
        name="exchange",
    )(*operands)


def mm(a, b, dims=((1,), (0,))):
    return lax.dot_general(a, b, (dims, ((), ())), precision=lax.Precision.HIGHEST, preferred_element_type=jnp.float32)


def eliminate(a):
    n = a.shape[0]
    w = 8
    lane = lax.broadcasted_iota(jnp.int32, (w, n), 1)
    sub = lax.broadcasted_iota(jnp.int32, (w, n), 0)
    rows = [a[w * h : w * h + w] for h in range(n // w)]

    def spread(x):
        return jnp.broadcast_to(x, (w, n))

    for g in range(n // w):
        at = g * w
        col = [spread(rows[g][:, at + k : at + k + 1]) for k in range(w)]
        row = rows[g]
        pivots, splats = [], []
        for k in range(w):
            inv = 1.0 / spread(col[k][k : k + 1])
            pivot = jnp.where(lane == at + k, inv, spread(row[k : k + 1]) * inv)
            pivots.append(jnp.where((lane > at + k) & (lane < at + w), 0.0, pivot))
            splats.append({j: spread(col[j][k : k + 1]) * inv for j in range(k + 1, w)})
            if k < w - 1:
                m = jnp.where(sub > k, col[k], 0.0)
                row = jnp.where((lane == at + k) & (sub > k), 0.0, row) - m * pivot
                for j in range(k + 1, w):
                    col[j] = col[j] - m * splats[k][j]
        rows[g] = row
        inside = (lane >= at) & (lane < at + w)
        for h in range(g + 1, n // w):
            c = [spread(rows[h][:, at + k : at + k + 1]) for k in range(w)]
            out = jnp.where(inside, 0.0, rows[h])
            for k in range(w):
                for j in range(k + 1, w):
                    c[j] = c[j] - c[k] * splats[k][j]
            for k in range(w):
                out = out - c[k] * pivots[k]
            rows[h] = out
    upper, inverse = [], []
    for h in range(n // w):
        at = sub + w * h
        scale = lax.rsqrt(spread(jnp.sum(jnp.where(lane == at, rows[h], 0.0), axis=1, keepdims=True)))
        upper.append(jnp.where(lane >= at, rows[h] * scale, 0.0))
        inverse.append(jnp.where(lane == at, scale, jnp.where(lane < at, rows[h] * scale, 0.0)))
    return jnp.concatenate(upper, axis=0), jnp.concatenate(inverse, axis=0)

def whiten_kernel(
    pieces, stacked_ref, factor_hbm, whitened_hbm,
    gram_ref, factor_ref, whitened_ref, sem,
):
    half = gram_ref.shape[1]
    long, short = half // pieces.shape[1], half // CORES // pieces.shape[1]
    first_out = pltpu.make_async_copy(whitened_ref.at[:half], whitened_hbm.at[:half], sem.at[0])
    second_out = pltpu.make_async_copy(whitened_ref.at[half:], whitened_hbm.at[half:], sem.at[1])
    factor_out = pltpu.make_async_copy(factor_ref, factor_hbm, sem.at[2])
    for c in range(CORES):
        for i in range(pieces.shape[1]):
            gram_ref[c, i * long : (i + 1) * long] = pieces[c, i, :long]
            at = c * (half // CORES) + i * short
            gram_ref[CORES, at : at + short] = pieces[c, i, long:]
    r11, i11 = eliminate(gram_ref[0])
    r12 = mm(i11, gram_ref[1])
    factor_ref[:half, :half] = r11
    factor_ref[:half, half:] = r12
    factor_ref[half:, :half] = jnp.zeros((half, half), jnp.float32)
    rest = gram_ref[2] - mm(r12, r12, ((0,), (0,)))
    first = mm(i11, stacked_ref[:half])
    whitened_ref[:half] = first
    first_out.start()
    left = stacked_ref[half:] - mm(r12, first, ((0,), (0,)))
    r22, i22 = eliminate(rest)
    factor_ref[half:, half:] = r22
    factor_out.start()
    whitened_ref[half:] = mm(i22, left)
    second_out.start()
    first_out.wait()
    factor_out.wait()
    second_out.wait()


def whiten(gram, stacked):
    vmem, hbm = pl.BlockSpec(memory_space=pltpu.VMEM), pl.BlockSpec(memory_space=pltpu.HBM)
    factor_shape = (stacked.shape[0],) * 2
    return pl.pallas_call(
        whiten_kernel,
        out_shape=(
            jax.ShapeDtypeStruct(factor_shape, jnp.float32),
            jax.ShapeDtypeStruct(stacked.shape, jnp.float32),
        ),
        in_specs=[vmem, vmem],
        out_specs=(hbm, hbm),
        scratch_shapes=[
            pltpu.VMEM((CORES + 1, gram.shape[3], gram.shape[3]), jnp.float32),
            pltpu.VMEM(factor_shape, jnp.float32),
            pltpu.VMEM(stacked.shape, jnp.float32),
            pltpu.SemaphoreType.DMA((3,)),
        ],
        compiler_params=pltpu.CompilerParams(vmem_limit_bytes=VMEM_BYTES),
        name="whiten",
    )(gram, stacked)


def solution(mesh):
    n_grp, n_lev = mesh.shape["grp"], mesh.shape["lev"]

    def on_device(ocean_field, climatology, land_mask, bottom_index, vertical_modes):
        stacked, gram = exchange(
            n_grp, n_lev, ocean_field, climatology, land_mask, bottom_index, vertical_modes
        )
        return whiten(gram, stacked)

    in_specs = (
        P(None, "lev", "grp"),
        P(None, ("grp", "lev")),
        P(("grp", "lev")),
        P(("grp", "lev")),
        P(),
    )
    out_specs = (P(), P(None, ("grp", "lev")))
    return jax.shard_map(
        on_device, mesh=mesh, in_specs=in_specs, out_specs=out_specs, check_vma=False
    )
```

```python
import functools

import jax
import jax.numpy as jnp
from jax import lax
from jax.experimental import pallas as pl
from jax.experimental.pallas import tpu as pltpu
from jax.sharding import PartitionSpec as P

MESH = pl.DeviceIdType.MESH
DAYS = 16
MODES = 16
LANES = 128
VMEM_BYTES = 40 * 1024 * 1024
CORES = 2
N_X = 4
SIDES = (1, -1)
PARTS = 2


def exchange_kernel(
    n_grp, n_lev,
    ocean_ref, clim_hbm, mask_hbm, bottom_hbm, modes_hbm,
    stacked_ref, gram_ref,
    clim_ref, mask_ref, bottom_ref, modes_ref,
    recv, clim_rows, limit_rows, weights, turned, anomaly, water_clim,
    limit_out, limit_in, q_out, q_in, sums_out, sums_in, theirs, packed, pair_buf, rs_buf, sum_buf, gather_buf,
    in_sem, local_sem, a_send, a_recv, l_sem, q_sem, t_sem, p_sem, r_send, r_recv, s_send, s_recv, g_send, g_recv,
):
    me_g = lax.axis_index("grp")
    me_l = lax.axis_index("lev")
    core = lax.rem(me_g, CORES)
    me_z = me_g // CORES
    n_z = n_grp // CORES
    n_y = n_lev // N_X
    slabs = clim_ref.shape[1] // LANES
    rows = 2 * slabs

    inputs = [
        pltpu.make_async_copy(src, dst, in_sem.at[i])
        for i, (src, dst) in enumerate(
            [(mask_hbm, mask_ref), (bottom_hbm, bottom_ref), (modes_hbm, modes_ref), (clim_hbm, clim_ref)]
        )
    ]
    for copy in inputs:
        copy.start()

    def far_first(n):
        return sorted(range(n), key=lambda d: -min(d, n - d))

    y_at = [lax.rem(me_l // N_X + d, n_y) * N_X for d in range(n_y)]
    x_at = [lax.rem(lax.rem(me_l, N_X) + d, N_X) for d in range(N_X)]

    def at(dy, dx):
        return y_at[dy % n_y] + x_at[dx % N_X]

    steps = [(dy, dx) for dy in far_first(n_y) for dx in far_first(N_X)][:-1]
    peers = [at(dy, dx) for dy, dx in steps]
    senders = [at(-dy, -dx) for dy, dx in steps]

    reach = n_y // 2
    first_k = N_X // 2
    per_side = reach * N_X - first_k
    routes = [(i, 0, dx, 0) for i, dx in enumerate(far_first(N_X))]
    own_slots = len(routes)
    side_routes = []
    for k in range(first_k, reach * N_X):
        hops = reach - 1 - k // N_X
        for side, sign in enumerate(SIDES):
            dx = k % N_X if side == 0 else N_X - 1 - k % N_X
            slot = own_slots + side * per_side + k - first_k
            side_routes.append((slot, sign * hops, dx, sign * (hops + 1)))
    routes = side_routes + routes

    def z_to(o):
        return lax.rem(me_z + o, n_z)

    def z_from(o):
        return lax.rem(me_z + n_z - o, n_z)

    partner = (me_z * CORES + 1 - core, me_l)

    barrier = pltpu.get_barrier_semaphore()

    for peer in peers:
        pl.semaphore_signal(barrier, inc=1, device_id=(me_g, peer), device_id_type=MESH)
    for o in range(1, n_z):
        pl.semaphore_signal(
            barrier, inc=1, device_id=(z_to(o) * CORES + core, me_l), device_id_type=MESH
        )

    pl.semaphore_signal(barrier, inc=1, device_id=partner, device_id_type=MESH)
    pl.semaphore_wait(barrier, n_lev + n_z - 1)

    part_days = DAYS // PARTS

    def block_copy(part, owner, to, slot):
        days = pl.ds(part * part_days, part_days)
        return pltpu.make_async_remote_copy(
            src_ref=ocean_ref.at[days, pl.ds(pl.multiple_of(owner * rows, rows), rows), :],
            dst_ref=recv.at[slot, days],
            send_sem=a_send.at[part, slot],
            recv_sem=a_recv.at[part, slot],
            device_id=(me_g, to),
            device_id_type=MESH,
        )

    def send_blocks(part):
        for slot, hops, dx, dy in routes:
            if (hops, dx) != (0, 0):
                block_copy(part, at(dy, dx), at(hops, dx), slot).start()

    stay = [
        (slot, pltpu.make_async_copy(
            ocean_ref.at[:, pl.ds(pl.multiple_of(at(dy, dx) * rows, rows), rows), :],
            recv.at[slot], local_sem.at[i],
        ))
        for i, (slot, dy, dx) in enumerate(
            [(slot, dy, dx) for slot, hops, dx, dy in routes if (hops, dx) == (0, 0)]
        )
    ]

    send_blocks(0)
    for copy in inputs:
        copy.wait()
    for _, copy in stay:
        copy.start()

    def neighbour_copy(src, dst, sems, sign):
        return pltpu.make_async_remote_copy(
            src_ref=src, dst_ref=dst, send_sem=sems.at[0], recv_sem=sems.at[1],
            device_id=(me_g, at(sign, 0)), device_id_type=MESH,
        )

    limit_out[...] = jnp.where(mask_ref[...] == 1, bottom_ref[...], 0)
    limit_copies = [
        neighbour_copy(limit_out, limit_in.at[side], l_sem.at[side], -sign) for side, sign in enumerate(SIDES)
    ]
    for copy in limit_copies:
        copy.start()

    def spread_limit(limit, k):
        for slab in range(slabs):
            limit_rows[k, 2 * slab : 2 * slab + 1, :] = limit[slab : slab + 1, :]
            limit_rows[k, 2 * slab + 1 : 2 * slab + 2, :] = limit[slab : slab + 1, :] - 1

    spread_limit(limit_out[...], 2)

    for t in range(clim_ref.shape[0] // 8):
        block = clim_ref[8 * t : 8 * t + 8, :]
        for k in range(8):
            for slab in range(slabs):
                row = 2 * slab + k % 2
                clim_rows[4 * t + k // 2, row : row + 1, :] = block[
                    k : k + 1, slab * LANES : (slab + 1) * LANES
                ]

    width = slabs * MODES
    depth = n_lev * rows
    levels = modes_ref.shape[1]
    q = lax.broadcasted_iota(jnp.int32, (depth, levels), 0)
    l = lax.broadcasted_iota(jnp.int32, (depth, levels), 1)
    spread_levels = jnp.where(2 * (q // rows) + lax.rem(q, 2) == l, 1.0, 0.0).astype(jnp.bfloat16)
    m = lax.broadcasted_iota(jnp.int32, (MODES, width), 0)
    r = lax.broadcasted_iota(jnp.int32, (MODES, width), 1)
    spread_modes = jnp.where(lax.rem(r, MODES) == m, 1.0, 0.0).astype(jnp.bfloat16)
    tall = lax.dot_general(
        spread_levels, modes_ref[...], (((1,), (1,)), ((), ())), preferred_element_type=jnp.float32
    ).astype(jnp.bfloat16)
    wide = jnp.dot(tall, spread_modes, preferred_element_type=jnp.float32)
    q = lax.broadcasted_iota(jnp.int32, (depth, width), 0)
    r = lax.broadcasted_iota(jnp.int32, (depth, width), 1)
    wide = jnp.where(r // MODES == lax.rem(q, rows) // 2, wide, 0.0)
    weights[...] = wide.astype(jnp.bfloat16)

    for s in range(n_lev):
        water_clim[s * rows : (s + 1) * rows] = jnp.where(limit_rows[2] > 2 * s, clim_rows[s], 0.0)
    source = q // rows
    dy = lax.rem(me_l // N_X + n_y - source // N_X, n_y)
    dx = lax.rem(lax.rem(me_l, N_X) + N_X - lax.rem(source, N_X), N_X)
    below = ((dy > 0) & (dy < reach)) | ((dy == reach) & (dx >= first_k))
    above = (dy > reach) | ((dy == reach) & (dx < first_k))
    q_copies = []
    for side, sign in enumerate(SIDES):
        q_out[side] = lax.dot_general(
            jnp.where(above if side else below, wide, 0.0), water_clim[...], (((0,), (0,)), ((), ())),
            precision=lax.Precision.HIGHEST, preferred_element_type=jnp.float32,
        )
        q_copies.append(neighbour_copy(q_out.at[side], q_in.at[side], q_sem.at[side], -sign))
        q_copies[-1].start()

    for part in range(1, PARTS):
        send_blocks(part)

    for slot, hops, dx, dy in routes:
        s = at(-hops, -dx)
        turned[slot * rows : (slot + 1) * rows] = weights[pl.ds(pl.multiple_of(s * rows, rows), rows)]

    for copy in limit_copies:
        copy.wait_recv()
    for side in range(2):
        spread_limit(limit_in[side], side)

    def use(part, slot, s, kind):
        water = limit_rows[kind] > 2 * s
        for d in range(part * part_days, (part + 1) * part_days):
            value = recv[slot, d].astype(jnp.float32)
            if kind == 2:
                value = value - clim_rows[s]
            anomaly[pl.ds(pl.multiple_of(slot * rows, rows), rows), d * LANES : (d + 1) * LANES] = jnp.where(
                water, value, 0.0
            ).astype(jnp.bfloat16)

    def project(first, count, part, parts):
        span = slice(first * rows, (first + count) * rows)
        lanes = DAYS // parts * LANES
        return lax.dot_general(
            turned[span], anomaly[span, part * lanes : (part + 1) * lanes], (((0,), (0,)), ((), ())),
            preferred_element_type=jnp.float32,
        )

    for _, copy in stay:
        copy.wait()
    at_home = [slot - own_slots - side * per_side for side, slot in enumerate(sorted(slot for slot, _ in stay)[1:])]
    sum_copies = []
    for part in range(PARTS):

        @pl.loop(0, per_side)
        def _(j):
            k = j + first_k
            hops, turn = reach - 1 - k // N_X, lax.rem(k, N_X)
            for side, sign in enumerate(SIDES):
                dx = turn if side == 0 else N_X - 1 - turn
                y = lax.rem(me_l // N_X + n_y - sign * hops, n_y)
                s = y * N_X + lax.rem(lax.rem(me_l, N_X) + N_X - dx, N_X)
                slot = own_slots + side * per_side + j

                @pl.when(j != at_home[side])
                def _():
                    block_copy(part, s, s, slot).wait_recv()

                use(part, slot, s, side)

        for side, sign in enumerate(SIDES):
            if part == 0:
                q_copies[side].wait_recv()
            total = project(own_slots + side * per_side, per_side, part, PARTS)
            for d in range(part_days):
                sums_out[side, part, d] = (
                    total[:, d * LANES : (d + 1) * LANES] - q_in[side]
                ).astype(jnp.bfloat16)
            sum_copies.append(
                neighbour_copy(sums_out.at[side, part], sums_in.at[side, part], t_sem.at[side, part], sign)
            )
            sum_copies[-1].start()

    for slot, hops, dx, dy in routes:
        if slot < own_slots:
            s = at(0, -dx)
            for part in range(PARTS):
                if dx:
                    block_copy(part, s, s, slot).wait_recv()
                use(part, slot, s, 2)
    coef = project(0, own_slots, 0, 1)
    for copy in sum_copies:
        copy.wait_recv()
    for d in range(DAYS):
        block = coef[:, d * LANES : (d + 1) * LANES]
        for side in range(2):
            block = block + sums_in[side, d // part_days, d % part_days].astype(jnp.float32)
        for slab in range(slabs):
            stacked_ref[d * MODES : (d + 1) * MODES, slab * LANES : (slab + 1) * LANES] = block[
                slab * MODES : (slab + 1) * MODES
            ]

    half = stacked_ref.shape[0] // 2
    share = half // CORES
    long, short = half // n_lev, share // n_lev

    def gram_block(x, y):
        return lax.dot_general(
            x, y, (((1,), (1,)), ((), ())),
            precision=lax.Precision.HIGHEST, preferred_element_type=jnp.float32,
        )

    def pack(c, out):
        row, rest = pl.multiple_of(c * half, half), pl.multiple_of(half + c * share, share)
        first = gram_block(stacked_ref[:half], stacked_ref[pl.ds(row, half)])
        last = gram_block(stacked_ref[pl.ds(rest, share)], stacked_ref[half:])
        for i in range(n_lev):
            out[i, :long] = first[i * long : (i + 1) * long]
            out[i, long:] = last[i * short : (i + 1) * short]

    def pair_copy(src, dst, k):
        return pltpu.make_async_remote_copy(
            src_ref=src, dst_ref=dst, send_sem=p_sem.at[k, 0], recv_sem=p_sem.at[k, 1],
            device_id=partner, device_id_type=MESH,
        )

    pack(1 - core, theirs)
    to_pair = pair_copy(theirs, pair_buf, 0)
    to_pair.start()
    pack(core, packed)
    to_pair.wait()
    packed[...] = packed[...] + pair_buf[...]

    def scatter_copy(to, slot, k):
        return pltpu.make_async_remote_copy(
            src_ref=packed.at[to], dst_ref=rs_buf.at[slot],
            send_sem=r_send.at[k], recv_sem=r_recv.at[k],
            device_id=(me_g, to), device_id_type=MESH,
        )

    for o, peer in enumerate(peers):
        scatter_copy(peer, me_l, o).start()

    rs_buf[me_l] = packed[me_l]

    for o, s in enumerate(senders):
        scatter_copy(s, s, o).wait_recv()

    sum_buf[me_z] = jnp.sum(rs_buf[...], axis=0)

    def sum_copy(to, slot, k):
        return pltpu.make_async_remote_copy(
            src_ref=sum_buf.at[me_z], dst_ref=sum_buf.at[slot],
            send_sem=s_send.at[k], recv_sem=s_recv.at[k],
            device_id=(to * CORES + core, me_l), device_id_type=MESH,
        )

    for o in range(1, n_z):
        sum_copy(z_to(o), me_z, o).start()
    for o in range(1, n_z):
        s = z_from(o)
        sum_copy(s, s, o).wait_recv()

    total_cols = clim_ref.shape[1] * n_grp * n_lev
    gather_buf[core, me_l] = jnp.sum(sum_buf[...], axis=0) * (1.0 / total_cols)

    def gather_copy(to, slot, k):
        return pltpu.make_async_remote_copy(
            src_ref=gather_buf.at[core, me_l], dst_ref=gather_buf.at[core, slot],
            send_sem=g_send.at[k], recv_sem=g_recv.at[k],
            device_id=(me_g, to), device_id_type=MESH,
        )

    for o, peer in enumerate(peers):
        gather_copy(peer, me_l, o).start()
    for o, s in enumerate(senders):
        gather_copy(s, s, o).wait_recv()

    to_pair = pair_copy(gather_buf.at[core], gather_buf.at[core], 1)
    to_pair.start()
    gram_ref[core] = gather_buf[core]
    to_pair.wait()
    gram_ref[1 - core] = gather_buf[1 - core]
    for o, peer in enumerate(peers):
        scatter_copy(peer, me_l, o).wait_send()
        gather_copy(peer, me_l, o).wait_send()
    for o in range(1, n_z):
        sum_copy(z_to(o), me_z, o).wait_send()
    for part in range(PARTS):
        for slot, hops, dx, dy in routes:
            if (hops, dx) != (0, 0):
                block_copy(part, at(dy, dx), at(hops, dx), slot).wait_send()
    for copy in limit_copies + q_copies + sum_copies:
        copy.wait_send()


def exchange(n_grp, n_lev, ocean, climatology, land_mask, bottom_index, modes):
    days, levels_dev, cols_grp = ocean.shape
    col_dev = climatology.shape[1]
    slabs = col_dev // LANES
    rows = levels_dev * slabs
    width = DAYS * MODES
    half = width // 2
    piece = (half + half // CORES) // n_lev
    tiles = cols_grp // LANES
    ocean = ocean.reshape(days, levels_dev, tiles, LANES).transpose(0, 2, 1, 3)
    ocean = ocean.reshape(days, tiles * levels_dev, LANES)
    vmem, hbm = pl.BlockSpec(memory_space=pltpu.VMEM), pl.BlockSpec(memory_space=pltpu.HBM)
    operands = (
        ocean, climatology,
        land_mask.reshape(slabs, LANES), bottom_index.reshape(slabs, LANES), modes,
    )
    operands = [pltpu.with_memory_space_constraint(x, pltpu.HBM) for x in operands]
    return pl.pallas_call(
        functools.partial(exchange_kernel, n_grp, n_lev),
        out_shape=(
            jax.ShapeDtypeStruct((width, col_dev), jnp.float32),
            jax.ShapeDtypeStruct((CORES, n_lev, piece, half), jnp.float32),
        ),
        in_specs=[hbm] * 5,
        out_specs=(vmem, vmem),
        scratch_shapes=[
            pltpu.VMEM(climatology.shape, jnp.float32),
            pltpu.VMEM((slabs, LANES), jnp.int32),
            pltpu.VMEM((slabs, LANES), jnp.int32),
            pltpu.VMEM(modes.shape, jnp.bfloat16),
            pltpu.VMEM((n_lev, days, rows, LANES), jnp.bfloat16),
            pltpu.VMEM((n_lev, rows, LANES), jnp.float32),
            pltpu.VMEM((3, rows, LANES), jnp.int32),
            pltpu.VMEM((n_lev * rows, slabs * MODES), jnp.bfloat16),
            pltpu.VMEM((n_lev * rows, slabs * MODES), jnp.bfloat16),
            pltpu.VMEM((n_lev * rows, days * LANES), jnp.bfloat16),
            pltpu.VMEM((n_lev * rows, LANES), jnp.float32),
            pltpu.VMEM((slabs, LANES), jnp.int32),
            pltpu.VMEM((2, slabs, LANES), jnp.int32),
            pltpu.VMEM((2, slabs * MODES, LANES), jnp.float32),
            pltpu.VMEM((2, slabs * MODES, LANES), jnp.float32),
            pltpu.VMEM((2, PARTS, days // PARTS, slabs * MODES, LANES), jnp.bfloat16),
            pltpu.VMEM((2, PARTS, days // PARTS, slabs * MODES, LANES), jnp.bfloat16),
            pltpu.VMEM((n_lev, piece, half), jnp.float32),
            pltpu.VMEM((n_lev, piece, half), jnp.float32),
            pltpu.VMEM((n_lev, piece, half), jnp.float32),
            pltpu.VMEM((n_lev, piece, half), jnp.float32),
            pltpu.VMEM((n_grp // CORES, piece, half), jnp.float32),
            pltpu.VMEM((CORES, n_lev, piece, half), jnp.float32),
            pltpu.SemaphoreType.DMA((4,)),
            pltpu.SemaphoreType.DMA((3,)),
            pltpu.SemaphoreType.DMA((PARTS, n_lev)),
            pltpu.SemaphoreType.DMA((PARTS, n_lev)),
            pltpu.SemaphoreType.DMA((2, 2)),
            pltpu.SemaphoreType.DMA((2, 2)),
            pltpu.SemaphoreType.DMA((2, PARTS, 2)),
            pltpu.SemaphoreType.DMA((2, 2)),
            pltpu.SemaphoreType.DMA((n_lev,)),
            pltpu.SemaphoreType.DMA((n_lev,)),
            pltpu.SemaphoreType.DMA((n_grp // CORES,)),
            pltpu.SemaphoreType.DMA((n_grp // CORES,)),
            pltpu.SemaphoreType.DMA((n_lev,)),
            pltpu.SemaphoreType.DMA((n_lev,)),
        ],
        compiler_params=pltpu.CompilerParams(
            collective_id=0, has_side_effects=True, vmem_limit_bytes=VMEM_BYTES
        ),
        name="exchange",
    )(*operands)


def mm(a, b, dims=((1,), (0,))):
    return lax.dot_general(a, b, (dims, ((), ())), precision=lax.Precision.HIGHEST, preferred_element_type=jnp.float32)


def eliminate(a):
    n = a.shape[0]
    w = 8
    lane = lax.broadcasted_iota(jnp.int32, (w, n), 1)
    sub = lax.broadcasted_iota(jnp.int32, (w, n), 0)
    rows = [a[w * h : w * h + w] for h in range(n // w)]

    def spread(x):
        return jnp.broadcast_to(x, (w, n))

    for g in range(n // w):
        at = g * w
        col = [spread(rows[g][:, at + k : at + k + 1]) for k in range(w)]
        row = rows[g]
        pivots, splats = [], []
        for k in range(w):
            inv = 1.0 / spread(col[k][k : k + 1])
            pivot = jnp.where(lane == at + k, inv, spread(row[k : k + 1]) * inv)
            pivots.append(jnp.where((lane > at + k) & (lane < at + w), 0.0, pivot))
            splats.append({j: spread(col[j][k : k + 1]) * inv for j in range(k + 1, w)})
            if k < w - 1:
                m = jnp.where(sub > k, col[k], 0.0)
                row = jnp.where((lane == at + k) & (sub > k), 0.0, row) - m * pivot
                for j in range(k + 1, w):
                    col[j] = col[j] - m * splats[k][j]
        rows[g] = row
        inside = (lane >= at) & (lane < at + w)
        for h in range(g + 1, n // w):
            c = [spread(rows[h][:, at + k : at + k + 1]) for k in range(w)]
            out = jnp.where(inside, 0.0, rows[h])
            for k in range(w):
                for j in range(k + 1, w):
                    c[j] = c[j] - c[k] * splats[k][j]
            for k in range(w):
                out = out - c[k] * pivots[k]
            rows[h] = out
    upper, inverse = [], []
    for h in range(n // w):
        at = sub + w * h
        scale = lax.rsqrt(spread(jnp.sum(jnp.where(lane == at, rows[h], 0.0), axis=1, keepdims=True)))
        upper.append(jnp.where(lane >= at, rows[h] * scale, 0.0))
        inverse.append(jnp.where(lane == at, scale, jnp.where(lane < at, rows[h] * scale, 0.0)))
    return jnp.concatenate(upper, axis=0), jnp.concatenate(inverse, axis=0)

def whiten_kernel(
    pieces, stacked_ref, factor_hbm, whitened_hbm,
    gram_ref, factor_ref, whitened_ref, sem,
):
    half = gram_ref.shape[1]
    long, short = half // pieces.shape[1], half // CORES // pieces.shape[1]
    first_out = pltpu.make_async_copy(whitened_ref.at[:half], whitened_hbm.at[:half], sem.at[0])
    second_out = pltpu.make_async_copy(whitened_ref.at[half:], whitened_hbm.at[half:], sem.at[1])
    factor_out = pltpu.make_async_copy(factor_ref, factor_hbm, sem.at[2])
    for c in range(CORES):
        for i in range(pieces.shape[1]):
            gram_ref[c, i * long : (i + 1) * long] = pieces[c, i, :long]
            at = c * (half // CORES) + i * short
            gram_ref[CORES, at : at + short] = pieces[c, i, long:]
    r11, i11 = eliminate(gram_ref[0])
    r12 = mm(i11, gram_ref[1])
    factor_ref[:half, :half] = r11
    factor_ref[:half, half:] = r12
    factor_ref[half:, :half] = jnp.zeros((half, half), jnp.float32)
    rest = gram_ref[2] - mm(r12, r12, ((0,), (0,)))
    first = mm(i11, stacked_ref[:half])
    whitened_ref[:half] = first
    first_out.start()
    left = stacked_ref[half:] - mm(r12, first, ((0,), (0,)))
    r22, i22 = eliminate(rest)
    factor_ref[half:, half:] = r22
    factor_out.start()
    whitened_ref[half:] = mm(i22, left)
    second_out.start()
    first_out.wait()
    factor_out.wait()
    second_out.wait()


def whiten(gram, stacked):
    vmem, hbm = pl.BlockSpec(memory_space=pltpu.VMEM), pl.BlockSpec(memory_space=pltpu.HBM)
    factor_shape = (stacked.shape[0],) * 2
    return pl.pallas_call(
        whiten_kernel,
        out_shape=(
            jax.ShapeDtypeStruct(factor_shape, jnp.float32),
            jax.ShapeDtypeStruct(stacked.shape, jnp.float32),
        ),
        in_specs=[vmem, vmem],
        out_specs=(hbm, hbm),
        scratch_shapes=[
            pltpu.VMEM((CORES + 1, gram.shape[3], gram.shape[3]), jnp.float32),
            pltpu.VMEM(factor_shape, jnp.float32),
            pltpu.VMEM(stacked.shape, jnp.float32),
            pltpu.SemaphoreType.DMA((3,)),
        ],
        compiler_params=pltpu.CompilerParams(vmem_limit_bytes=VMEM_BYTES),
        name="whiten",
    )(gram, stacked)


def solution(mesh):
    n_grp, n_lev = mesh.shape["grp"], mesh.shape["lev"]

    def on_device(ocean_field, climatology, land_mask, bottom_index, vertical_modes):
        stacked, gram = exchange(
            n_grp, n_lev, ocean_field, climatology, land_mask, bottom_index, vertical_modes
        )
        return whiten(gram, stacked)

    in_specs = (
        P(None, "lev", "grp"),
        P(None, ("grp", "lev")),
        P(("grp", "lev")),
        P(("grp", "lev")),
        P(),
    )
    out_specs = (P(), P(None, ("grp", "lev")))
    return jax.shard_map(
        on_device, mesh=mesh, in_specs=in_specs, out_specs=out_specs, check_vma=False
    )
```

```python
import functools

import jax
import jax.numpy as jnp
from jax import lax
from jax.experimental import pallas as pl
from jax.experimental.pallas import tpu as pltpu
from jax.sharding import PartitionSpec as P

MESH = pl.DeviceIdType.MESH
DAYS = 16
MODES = 16
LANES = 128
VMEM_BYTES = 40 * 1024 * 1024
CORES = 2
N_X = 4
SIDES = (1, -1)
PARTS = 2


def exchange_kernel(
    n_grp, n_lev,
    ocean_ref, clim_hbm, mask_hbm, bottom_hbm, modes_hbm,
    stacked_ref, gram_ref,
    clim_ref, mask_ref, bottom_ref, modes_ref,
    recv, clim_rows, limit_rows, weights, turned, anomaly, water_clim,
    limit_out, limit_in, q_out, q_in, sums_out, sums_in, theirs, packed, pair_buf, rs_buf, sum_buf, gather_buf,
    in_sem, local_sem, a_send, a_recv, l_sem, q_sem, t_sem, p_sem, r_send, r_recv, s_send, s_recv, g_send, g_recv,
):
    me_g = lax.axis_index("grp")
    me_l = lax.axis_index("lev")
    core = lax.rem(me_g, CORES)
    me_z = me_g // CORES
    n_z = n_grp // CORES
    n_y = n_lev // N_X
    slabs = clim_ref.shape[1] // LANES
    rows = 2 * slabs

    inputs = [
        pltpu.make_async_copy(src, dst, in_sem.at[i])
        for i, (src, dst) in enumerate(
            [(mask_hbm, mask_ref), (bottom_hbm, bottom_ref), (modes_hbm, modes_ref), (clim_hbm, clim_ref)]
        )
    ]
    for copy in inputs:
        copy.start()

    def far_first(n):
        return sorted(range(n), key=lambda d: -min(d, n - d))

    y_at = [lax.rem(me_l // N_X + d, n_y) * N_X for d in range(n_y)]
    x_at = [lax.rem(lax.rem(me_l, N_X) + d, N_X) for d in range(N_X)]

    def at(dy, dx):
        return y_at[dy % n_y] + x_at[dx % N_X]

    steps = [(dy, dx) for dy in far_first(n_y) for dx in far_first(N_X)][:-1]
    peers = [at(dy, dx) for dy, dx in steps]
    senders = [at(-dy, -dx) for dy, dx in steps]

    reach = n_y // 2
    first_k = N_X // 2
    per_side = reach * N_X - first_k
    routes = [(i, 0, dx, 0) for i, dx in enumerate(far_first(N_X))]
    own_slots = len(routes)
    side_routes = []
    for k in range(first_k, reach * N_X):
        hops = reach - 1 - k // N_X
        for side, sign in enumerate(SIDES):
            dx = k % N_X if side == 0 else N_X - 1 - k % N_X
            slot = own_slots + side * per_side + k - first_k
            side_routes.append((slot, sign * hops, dx, sign * (hops + 1)))
    routes = side_routes + routes

    def z_to(o):
        return lax.rem(me_z + o, n_z)

    def z_from(o):
        return lax.rem(me_z + n_z - o, n_z)

    partner = (me_z * CORES + 1 - core, me_l)

    barrier = pltpu.get_barrier_semaphore()

    for peer in peers:
        pl.semaphore_signal(barrier, inc=1, device_id=(me_g, peer), device_id_type=MESH)
    for o in range(1, n_z):
        pl.semaphore_signal(
            barrier, inc=1, device_id=(z_to(o) * CORES + core, me_l), device_id_type=MESH
        )

    pl.semaphore_signal(barrier, inc=1, device_id=partner, device_id_type=MESH)
    pl.semaphore_wait(barrier, n_lev + n_z - 1)

    part_days = DAYS // PARTS

    def block_copy(part, owner, to, slot):
        days = pl.ds(part * part_days, part_days)
        return pltpu.make_async_remote_copy(
            src_ref=ocean_ref.at[days, pl.ds(pl.multiple_of(owner * rows, rows), rows), :],
            dst_ref=recv.at[slot, days],
            send_sem=a_send.at[part, slot],
            recv_sem=a_recv.at[part, slot],
            device_id=(me_g, to),
            device_id_type=MESH,
        )

    def send_blocks(part):
        for slot, hops, dx, dy in routes:
            if (hops, dx) != (0, 0):
                block_copy(part, at(dy, dx), at(hops, dx), slot).start()

    stay = [
        (slot, pltpu.make_async_copy(
            ocean_ref.at[:, pl.ds(pl.multiple_of(at(dy, dx) * rows, rows), rows), :],
            recv.at[slot], local_sem.at[i],
        ))
        for i, (slot, dy, dx) in enumerate(
            [(slot, dy, dx) for slot, hops, dx, dy in routes if (hops, dx) == (0, 0)]
        )
    ]

    send_blocks(0)
    for copy in inputs:
        copy.wait()
    for _, copy in stay:
        copy.start()

    def neighbour_copy(src, dst, sems, sign):
        return pltpu.make_async_remote_copy(
            src_ref=src, dst_ref=dst, send_sem=sems.at[0], recv_sem=sems.at[1],
            device_id=(me_g, at(sign, 0)), device_id_type=MESH,
        )

    limit_out[...] = jnp.where(mask_ref[...] == 1, bottom_ref[...], 0)
    limit_copies = [
        neighbour_copy(limit_out, limit_in.at[side], l_sem.at[side], -sign) for side, sign in enumerate(SIDES)
    ]
    for copy in limit_copies:
        copy.start()

    def spread_limit(limit, k):
        for slab in range(slabs):
            limit_rows[k, 2 * slab : 2 * slab + 1, :] = limit[slab : slab + 1, :]
            limit_rows[k, 2 * slab + 1 : 2 * slab + 2, :] = limit[slab : slab + 1, :] - 1

    spread_limit(limit_out[...], 2)

    for t in range(clim_ref.shape[0] // 8):
        block = clim_ref[8 * t : 8 * t + 8, :]
        for k in range(8):
            for slab in range(slabs):
                row = 2 * slab + k % 2
                clim_rows[4 * t + k // 2, row : row + 1, :] = block[
                    k : k + 1, slab * LANES : (slab + 1) * LANES
                ]

    width = slabs * MODES
    depth = n_lev * rows
    levels = modes_ref.shape[1]
    q = lax.broadcasted_iota(jnp.int32, (depth, levels), 0)
    l = lax.broadcasted_iota(jnp.int32, (depth, levels), 1)
    spread_levels = jnp.where(2 * (q // rows) + lax.rem(q, 2) == l, 1.0, 0.0).astype(jnp.bfloat16)
    m = lax.broadcasted_iota(jnp.int32, (MODES, width), 0)
    r = lax.broadcasted_iota(jnp.int32, (MODES, width), 1)
    spread_modes = jnp.where(lax.rem(r, MODES) == m, 1.0, 0.0).astype(jnp.bfloat16)
    tall = lax.dot_general(
        spread_levels, modes_ref[...], (((1,), (1,)), ((), ())), preferred_element_type=jnp.float32
    ).astype(jnp.bfloat16)
    wide = jnp.dot(tall, spread_modes, preferred_element_type=jnp.float32)
    q = lax.broadcasted_iota(jnp.int32, (depth, width), 0)
    r = lax.broadcasted_iota(jnp.int32, (depth, width), 1)
    wide = jnp.where(r // MODES == lax.rem(q, rows) // 2, wide, 0.0)
    weights[...] = wide.astype(jnp.bfloat16)

    for s in range(n_lev):
        water_clim[s * rows : (s + 1) * rows] = jnp.where(limit_rows[2] > 2 * s, clim_rows[s], 0.0)
    source = q // rows
    dy = lax.rem(me_l // N_X + n_y - source // N_X, n_y)
    dx = lax.rem(lax.rem(me_l, N_X) + N_X - lax.rem(source, N_X), N_X)
    below = ((dy > 0) & (dy < reach)) | ((dy == reach) & (dx >= first_k))
    above = (dy > reach) | ((dy == reach) & (dx < first_k))
    q_copies = []
    for side, sign in enumerate(SIDES):
        q_out[side] = lax.dot_general(
            jnp.where(above if side else below, wide, 0.0), water_clim[...], (((0,), (0,)), ((), ())),
            precision=lax.Precision.HIGHEST, preferred_element_type=jnp.float32,
        )
        q_copies.append(neighbour_copy(q_out.at[side], q_in.at[side], q_sem.at[side], -sign))
        q_copies[-1].start()

    for part in range(1, PARTS):
        send_blocks(part)

    for slot, hops, dx, dy in routes:
        s = at(-hops, -dx)
        turned[slot * rows : (slot + 1) * rows] = weights[pl.ds(pl.multiple_of(s * rows, rows), rows)]

    for copy in limit_copies:
        copy.wait_recv()
    for side in range(2):
        spread_limit(limit_in[side], side)

    def use(part, slot, s, kind):
        water = limit_rows[kind] > 2 * s
        for d in range(part * part_days, (part + 1) * part_days):
            value = recv[slot, d].astype(jnp.float32)
            if kind == 2:
                value = value - clim_rows[s]
            anomaly[pl.ds(pl.multiple_of(slot * rows, rows), rows), d * LANES : (d + 1) * LANES] = jnp.where(
                water, value, 0.0
            ).astype(jnp.bfloat16)

    def project(first, count, part, parts):
        span = slice(first * rows, (first + count) * rows)
        lanes = DAYS // parts * LANES
        return lax.dot_general(
            turned[span], anomaly[span, part * lanes : (part + 1) * lanes], (((0,), (0,)), ((), ())),
            preferred_element_type=jnp.float32,
        )

    for _, copy in stay:
        copy.wait()
    at_home = [slot - own_slots - side * per_side for side, slot in enumerate(sorted(slot for slot, _ in stay)[1:])]
    sum_copies = []
    for part in range(PARTS):

        @pl.loop(0, per_side)
        def _(j):
            k = j + first_k
            hops, turn = reach - 1 - k // N_X, lax.rem(k, N_X)
            for side, sign in enumerate(SIDES):
                dx = turn if side == 0 else N_X - 1 - turn
                y = lax.rem(me_l // N_X + n_y - sign * hops, n_y)
                s = y * N_X + lax.rem(lax.rem(me_l, N_X) + N_X - dx, N_X)
                slot = own_slots + side * per_side + j

                @pl.when(j != at_home[side])
                def _():
                    block_copy(part, s, s, slot).wait_recv()

                use(part, slot, s, side)

        for side, sign in enumerate(SIDES):
            if part == 0:
                q_copies[side].wait_recv()
            total = project(own_slots + side * per_side, per_side, part, PARTS)
            for d in range(part_days):
                sums_out[side, part, d] = (
                    total[:, d * LANES : (d + 1) * LANES] - q_in[side]
                ).astype(jnp.bfloat16)
            sum_copies.append(
                neighbour_copy(sums_out.at[side, part], sums_in.at[side, part], t_sem.at[side, part], sign)
            )
            sum_copies[-1].start()

    for slot, hops, dx, dy in routes:
        if slot < own_slots:
            s = at(0, -dx)
            for part in range(PARTS):
                if dx:
                    block_copy(part, s, s, slot).wait_recv()
                use(part, slot, s, 2)
    coef = project(0, own_slots, 0, 1)
    for part in range(PARTS):
        for slot, hops, dx, dy in routes:
            if (hops, dx) != (0, 0):
                block_copy(part, at(dy, dx), at(hops, dx), slot).wait_send()
    for copy in limit_copies + q_copies + sum_copies:
        copy.wait_send()
    for copy in sum_copies:
        copy.wait_recv()
    for d in range(DAYS):
        block = coef[:, d * LANES : (d + 1) * LANES]
        for side in range(2):
            block = block + sums_in[side, d // part_days, d % part_days].astype(jnp.float32)
        for slab in range(slabs):
            stacked_ref[d * MODES : (d + 1) * MODES, slab * LANES : (slab + 1) * LANES] = block[
                slab * MODES : (slab + 1) * MODES
            ]

    half = stacked_ref.shape[0] // 2
    share = half // CORES
    long, short = half // n_lev, share // n_lev

    def gram_block(x, y):
        return lax.dot_general(
            x, y, (((1,), (1,)), ((), ())),
            precision=lax.Precision.HIGHEST, preferred_element_type=jnp.float32,
        )

    def pack(c, out):
        row, rest = pl.multiple_of(c * half, half), pl.multiple_of(half + c * share, share)
        first = gram_block(stacked_ref[:half], stacked_ref[pl.ds(row, half)])
        last = gram_block(stacked_ref[pl.ds(rest, share)], stacked_ref[half:])
        for i in range(n_lev):
            out[i, :long] = first[i * long : (i + 1) * long]
            out[i, long:] = last[i * short : (i + 1) * short]

    def pair_copy(src, dst, k):
        return pltpu.make_async_remote_copy(
            src_ref=src, dst_ref=dst, send_sem=p_sem.at[k, 0], recv_sem=p_sem.at[k, 1],
            device_id=partner, device_id_type=MESH,
        )

    pack(1 - core, theirs)
    to_pair = pair_copy(theirs, pair_buf, 0)
    to_pair.start()
    pack(core, packed)
    to_pair.wait()
    packed[...] = packed[...] + pair_buf[...]

    def scatter_copy(to, slot, k):
        return pltpu.make_async_remote_copy(
            src_ref=packed.at[to], dst_ref=rs_buf.at[slot],
            send_sem=r_send.at[k], recv_sem=r_recv.at[k],
            device_id=(me_g, to), device_id_type=MESH,
        )

    for o, peer in enumerate(peers):
        scatter_copy(peer, me_l, o).start()

    rs_buf[me_l] = packed[me_l]

    for o, s in enumerate(senders):
        scatter_copy(s, s, o).wait_recv()

    sum_buf[me_z] = jnp.sum(rs_buf[...], axis=0)

    def sum_copy(to, slot, k):
        return pltpu.make_async_remote_copy(
            src_ref=sum_buf.at[me_z], dst_ref=sum_buf.at[slot],
            send_sem=s_send.at[k], recv_sem=s_recv.at[k],
            device_id=(to * CORES + core, me_l), device_id_type=MESH,
        )

    for o in range(1, n_z):
        sum_copy(z_to(o), me_z, o).start()
    for o, peer in enumerate(peers):
        scatter_copy(peer, me_l, o).wait_send()
    for o in range(1, n_z):
        s = z_from(o)
        sum_copy(s, s, o).wait_recv()

    total_cols = clim_ref.shape[1] * n_grp * n_lev
    gather_buf[core, me_l] = jnp.sum(sum_buf[...], axis=0) * (1.0 / total_cols)

    def gather_copy(to, slot, k):
        return pltpu.make_async_remote_copy(
            src_ref=gather_buf.at[core, me_l], dst_ref=gather_buf.at[core, slot],
            send_sem=g_send.at[k], recv_sem=g_recv.at[k],
            device_id=(me_g, to), device_id_type=MESH,
        )

    for o, peer in enumerate(peers):
        gather_copy(peer, me_l, o).start()
    for o in range(1, n_z):
        sum_copy(z_to(o), me_z, o).wait_send()
    for o, s in enumerate(senders):
        gather_copy(s, s, o).wait_recv()

    to_pair = pair_copy(gather_buf.at[core], gather_buf.at[core], 1)
    to_pair.start()
    gram_ref[core] = gather_buf[core]
    for o, peer in enumerate(peers):
        gather_copy(peer, me_l, o).wait_send()
    to_pair.wait()
    gram_ref[1 - core] = gather_buf[1 - core]


def exchange(n_grp, n_lev, ocean, climatology, land_mask, bottom_index, modes):
    days, levels_dev, cols_grp = ocean.shape
    col_dev = climatology.shape[1]
    slabs = col_dev // LANES
    rows = levels_dev * slabs
    width = DAYS * MODES
    half = width // 2
    piece = (half + half // CORES) // n_lev
    tiles = cols_grp // LANES
    ocean = ocean.reshape(days, levels_dev, tiles, LANES).transpose(0, 2, 1, 3)
    ocean = ocean.reshape(days, tiles * levels_dev, LANES)
    vmem, hbm = pl.BlockSpec(memory_space=pltpu.VMEM), pl.BlockSpec(memory_space=pltpu.HBM)
    operands = (
        ocean, climatology,
        land_mask.reshape(slabs, LANES), bottom_index.reshape(slabs, LANES), modes,
    )
    operands = [pltpu.with_memory_space_constraint(x, pltpu.HBM) for x in operands]
    return pl.pallas_call(
        functools.partial(exchange_kernel, n_grp, n_lev),
        out_shape=(
            jax.ShapeDtypeStruct((width, col_dev), jnp.float32),
            jax.ShapeDtypeStruct((CORES, n_lev, piece, half), jnp.float32),
        ),
        in_specs=[hbm] * 5,
        out_specs=(vmem, vmem),
        scratch_shapes=[
            pltpu.VMEM(climatology.shape, jnp.float32),
            pltpu.VMEM((slabs, LANES), jnp.int32),
            pltpu.VMEM((slabs, LANES), jnp.int32),
            pltpu.VMEM(modes.shape, jnp.bfloat16),
            pltpu.VMEM((n_lev, days, rows, LANES), jnp.bfloat16),
            pltpu.VMEM((n_lev, rows, LANES), jnp.float32),
            pltpu.VMEM((3, rows, LANES), jnp.int32),
            pltpu.VMEM((n_lev * rows, slabs * MODES), jnp.bfloat16),
            pltpu.VMEM((n_lev * rows, slabs * MODES), jnp.bfloat16),
            pltpu.VMEM((n_lev * rows, days * LANES), jnp.bfloat16),
            pltpu.VMEM((n_lev * rows, LANES), jnp.float32),
            pltpu.VMEM((slabs, LANES), jnp.int32),
            pltpu.VMEM((2, slabs, LANES), jnp.int32),
            pltpu.VMEM((2, slabs * MODES, LANES), jnp.float32),
            pltpu.VMEM((2, slabs * MODES, LANES), jnp.float32),
            pltpu.VMEM((2, PARTS, days // PARTS, slabs * MODES, LANES), jnp.bfloat16),
            pltpu.VMEM((2, PARTS, days // PARTS, slabs * MODES, LANES), jnp.bfloat16),
            pltpu.VMEM((n_lev, piece, half), jnp.float32),
            pltpu.VMEM((n_lev, piece, half), jnp.float32),
            pltpu.VMEM((n_lev, piece, half), jnp.float32),
            pltpu.VMEM((n_lev, piece, half), jnp.float32),
            pltpu.VMEM((n_grp // CORES, piece, half), jnp.float32),
            pltpu.VMEM((CORES, n_lev, piece, half), jnp.float32),
            pltpu.SemaphoreType.DMA((4,)),
            pltpu.SemaphoreType.DMA((3,)),
            pltpu.SemaphoreType.DMA((PARTS, n_lev)),
            pltpu.SemaphoreType.DMA((PARTS, n_lev)),
            pltpu.SemaphoreType.DMA((2, 2)),
            pltpu.SemaphoreType.DMA((2, 2)),
            pltpu.SemaphoreType.DMA((2, PARTS, 2)),
            pltpu.SemaphoreType.DMA((2, 2)),
            pltpu.SemaphoreType.DMA((n_lev,)),
            pltpu.SemaphoreType.DMA((n_lev,)),
            pltpu.SemaphoreType.DMA((n_grp // CORES,)),
            pltpu.SemaphoreType.DMA((n_grp // CORES,)),
            pltpu.SemaphoreType.DMA((n_lev,)),
            pltpu.SemaphoreType.DMA((n_lev,)),
        ],
        compiler_params=pltpu.CompilerParams(
            collective_id=0, has_side_effects=True, vmem_limit_bytes=VMEM_BYTES
        ),
        name="exchange",
    )(*operands)


def mm(a, b, dims=((1,), (0,))):
    return lax.dot_general(a, b, (dims, ((), ())), precision=lax.Precision.HIGHEST, preferred_element_type=jnp.float32)


def eliminate(a):
    n = a.shape[0]
    w = 8
    lane = lax.broadcasted_iota(jnp.int32, (w, n), 1)
    sub = lax.broadcasted_iota(jnp.int32, (w, n), 0)
    rows = [a[w * h : w * h + w] for h in range(n // w)]

    def spread(x):
        return jnp.broadcast_to(x, (w, n))

    for g in range(n // w):
        at = g * w
        col = [spread(rows[g][:, at + k : at + k + 1]) for k in range(w)]
        row = rows[g]
        pivots, splats = [], []
        for k in range(w):
            inv = 1.0 / spread(col[k][k : k + 1])
            pivot = jnp.where(lane == at + k, inv, spread(row[k : k + 1]) * inv)
            pivots.append(jnp.where((lane > at + k) & (lane < at + w), 0.0, pivot))
            splats.append({j: spread(col[j][k : k + 1]) * inv for j in range(k + 1, w)})
            if k < w - 1:
                m = jnp.where(sub > k, col[k], 0.0)
                row = jnp.where((lane == at + k) & (sub > k), 0.0, row) - m * pivot
                for j in range(k + 1, w):
                    col[j] = col[j] - m * splats[k][j]
        rows[g] = row
        inside = (lane >= at) & (lane < at + w)
        for h in range(g + 1, n // w):
            c = [spread(rows[h][:, at + k : at + k + 1]) for k in range(w)]
            out = jnp.where(inside, 0.0, rows[h])
            for k in range(w):
                for j in range(k + 1, w):
                    c[j] = c[j] - c[k] * splats[k][j]
            for k in range(w):
                out = out - c[k] * pivots[k]
            rows[h] = out
    upper, inverse = [], []
    for h in range(n // w):
        at = sub + w * h
        scale = lax.rsqrt(spread(jnp.sum(jnp.where(lane == at, rows[h], 0.0), axis=1, keepdims=True)))
        upper.append(jnp.where(lane >= at, rows[h] * scale, 0.0))
        inverse.append(jnp.where(lane == at, scale, jnp.where(lane < at, rows[h] * scale, 0.0)))
    return jnp.concatenate(upper, axis=0), jnp.concatenate(inverse, axis=0)

def whiten_kernel(
    pieces, stacked_ref, factor_hbm, whitened_hbm,
    gram_ref, factor_ref, whitened_ref, sem,
):
    half = gram_ref.shape[1]
    long, short = half // pieces.shape[1], half // CORES // pieces.shape[1]
    first_out = pltpu.make_async_copy(whitened_ref.at[:half], whitened_hbm.at[:half], sem.at[0])
    cols = whitened_ref.shape[1] // 2
    second_out = [
        pltpu.make_async_copy(
            whitened_ref.at[half:, i * cols : (i + 1) * cols],
            whitened_hbm.at[half:, i * cols : (i + 1) * cols],
            sem.at[1 + i],
        )
        for i in range(2)
    ]
    factor_out = pltpu.make_async_copy(factor_ref, factor_hbm, sem.at[3])
    for c in range(CORES):
        for i in range(pieces.shape[1]):
            gram_ref[c, i * long : (i + 1) * long] = pieces[c, i, :long]
            at = c * (half // CORES) + i * short
            gram_ref[CORES, at : at + short] = pieces[c, i, long:]
    r11, i11 = eliminate(gram_ref[0])
    r12 = mm(i11, gram_ref[1])
    factor_ref[:half, :half] = r11
    factor_ref[:half, half:] = r12
    factor_ref[half:, :half] = jnp.zeros((half, half), jnp.float32)
    rest = gram_ref[2] - mm(r12, r12, ((0,), (0,)))
    first = mm(i11, stacked_ref[:half])
    whitened_ref[:half] = first
    first_out.start()
    left = stacked_ref[half:] - mm(r12, first, ((0,), (0,)))
    r22, i22 = eliminate(rest)
    factor_ref[half:, half:] = r22
    factor_out.start()
    for i in range(2):
        whitened_ref[half:, i * cols : (i + 1) * cols] = mm(i22, left[:, i * cols : (i + 1) * cols])
        second_out[i].start()
    first_out.wait()
    factor_out.wait()
    for i in range(2):
        second_out[i].wait()


def whiten(gram, stacked):
    vmem, hbm = pl.BlockSpec(memory_space=pltpu.VMEM), pl.BlockSpec(memory_space=pltpu.HBM)
    factor_shape = (stacked.shape[0],) * 2
    return pl.pallas_call(
        whiten_kernel,
        out_shape=(
            jax.ShapeDtypeStruct(factor_shape, jnp.float32),
            jax.ShapeDtypeStruct(stacked.shape, jnp.float32),
        ),
        in_specs=[vmem, vmem],
        out_specs=(hbm, hbm),
        scratch_shapes=[
            pltpu.VMEM((CORES + 1, gram.shape[3], gram.shape[3]), jnp.float32),
            pltpu.VMEM(factor_shape, jnp.float32),
            pltpu.VMEM(stacked.shape, jnp.float32),
            pltpu.SemaphoreType.DMA((4,)),
        ],
        compiler_params=pltpu.CompilerParams(vmem_limit_bytes=VMEM_BYTES),
        name="whiten",
    )(gram, stacked)


def solution(mesh):
    n_grp, n_lev = mesh.shape["grp"], mesh.shape["lev"]

    def on_device(ocean_field, climatology, land_mask, bottom_index, vertical_modes):
        stacked, gram = exchange(
            n_grp, n_lev, ocean_field, climatology, land_mask, bottom_index, vertical_modes
        )
        return whiten(gram, stacked)

    in_specs = (
        P(None, "lev", "grp"),
        P(None, ("grp", "lev")),
        P(("grp", "lev")),
        P(("grp", "lev")),
        P(),
    )
    out_specs = (P(), P(None, ("grp", "lev")))
    return jax.shard_map(
        on_device, mesh=mesh, in_specs=in_specs, out_specs=out_specs, check_vma=False
    )
```

```python
import functools

import jax
import jax.numpy as jnp
from jax import lax
from jax.experimental import pallas as pl
from jax.experimental.pallas import tpu as pltpu
from jax.sharding import PartitionSpec as P

MESH = pl.DeviceIdType.MESH
DAYS = 16
MODES = 16
LANES = 128
VMEM_BYTES = 40 * 1024 * 1024
CORES = 2
N_X = 4
SIDES = (1, -1)
PARTS = 2


def exchange_kernel(
    n_grp, n_lev,
    ocean_ref, clim_hbm, mask_hbm, bottom_hbm, modes_hbm,
    stacked_ref, gram_ref,
    clim_ref, mask_ref, bottom_ref, modes_ref,
    recv, clim_rows, limit_rows, weights, turned, anomaly, water_clim,
    limit_out, limit_in, q_out, q_in, sums_out, sums_in, theirs, packed, pair_buf, rs_buf, sum_buf, gather_buf,
    in_sem, local_sem, a_send, a_recv, l_sem, q_sem, t_sem, p_sem, r_send, r_recv, s_send, s_recv, g_send, g_recv,
):
    me_g = lax.axis_index("grp")
    me_l = lax.axis_index("lev")
    core = lax.rem(me_g, CORES)
    me_z = me_g // CORES
    n_z = n_grp // CORES
    n_y = n_lev // N_X
    slabs = clim_ref.shape[1] // LANES
    rows = 2 * slabs

    inputs = [
        pltpu.make_async_copy(src, dst, in_sem.at[i])
        for i, (src, dst) in enumerate(
            [(mask_hbm, mask_ref), (bottom_hbm, bottom_ref), (modes_hbm, modes_ref), (clim_hbm, clim_ref)]
        )
    ]
    for copy in inputs:
        copy.start()

    def far_first(n):
        return sorted(range(n), key=lambda d: -min(d, n - d))

    y_at = [lax.rem(me_l // N_X + d, n_y) * N_X for d in range(n_y)]
    x_at = [lax.rem(lax.rem(me_l, N_X) + d, N_X) for d in range(N_X)]

    def at(dy, dx):
        return y_at[dy % n_y] + x_at[dx % N_X]

    steps = [(dy, dx) for dy in far_first(n_y) for dx in far_first(N_X)][:-1]
    peers = [at(dy, dx) for dy, dx in steps]
    senders = [at(-dy, -dx) for dy, dx in steps]

    reach = n_y // 2
    first_k = N_X // 2
    per_side = reach * N_X - first_k
    routes = [(i, 0, dx, 0) for i, dx in enumerate(far_first(N_X))]
    own_slots = len(routes)
    side_routes = []
    for k in range(first_k, reach * N_X):
        hops = reach - 1 - k // N_X
        for side, sign in enumerate(SIDES):
            dx = k % N_X if side == 0 else N_X - 1 - k % N_X
            slot = own_slots + side * per_side + k - first_k
            side_routes.append((slot, sign * hops, dx, sign * (hops + 1)))
    routes = side_routes + routes

    def z_to(o):
        return lax.rem(me_z + o, n_z)

    def z_from(o):
        return lax.rem(me_z + n_z - o, n_z)

    partner = (me_z * CORES + 1 - core, me_l)

    barrier = pltpu.get_barrier_semaphore()

    for peer in peers:
        pl.semaphore_signal(barrier, inc=1, device_id=(me_g, peer), device_id_type=MESH)
    for o in range(1, n_z):
        pl.semaphore_signal(
            barrier, inc=1, device_id=(z_to(o) * CORES + core, me_l), device_id_type=MESH
        )

    pl.semaphore_signal(barrier, inc=1, device_id=partner, device_id_type=MESH)
    pl.semaphore_wait(barrier, n_lev + n_z - 1)

    part_days = DAYS // PARTS

    def block_copy(part, owner, to, slot):
        days = pl.ds(part * part_days, part_days)
        return pltpu.make_async_remote_copy(
            src_ref=ocean_ref.at[days, pl.ds(pl.multiple_of(owner * rows, rows), rows), :],
            dst_ref=recv.at[slot, days],
            send_sem=a_send.at[part, slot],
            recv_sem=a_recv.at[part, slot],
            device_id=(me_g, to),
            device_id_type=MESH,
        )

    def send_blocks(part):
        for slot, hops, dx, dy in routes:
            if (hops, dx) != (0, 0):
                block_copy(part, at(dy, dx), at(hops, dx), slot).start()

    stay = [
        (slot, pltpu.make_async_copy(
            ocean_ref.at[:, pl.ds(pl.multiple_of(at(dy, dx) * rows, rows), rows), :],
            recv.at[slot], local_sem.at[i],
        ))
        for i, (slot, dy, dx) in enumerate(
            [(slot, dy, dx) for slot, hops, dx, dy in routes if (hops, dx) == (0, 0)]
        )
    ]

    send_blocks(0)
    for copy in inputs:
        copy.wait()
    for _, copy in stay:
        copy.start()

    def neighbour_copy(src, dst, sems, sign):
        return pltpu.make_async_remote_copy(
            src_ref=src, dst_ref=dst, send_sem=sems.at[0], recv_sem=sems.at[1],
            device_id=(me_g, at(sign, 0)), device_id_type=MESH,
        )

    limit_out[...] = jnp.where(mask_ref[...] == 1, bottom_ref[...], 0)
    limit_copies = [
        neighbour_copy(limit_out, limit_in.at[side], l_sem.at[side], -sign) for side, sign in enumerate(SIDES)
    ]
    for copy in limit_copies:
        copy.start()

    def spread_limit(limit, k):
        for slab in range(slabs):
            limit_rows[k, 2 * slab : 2 * slab + 1, :] = limit[slab : slab + 1, :]
            limit_rows[k, 2 * slab + 1 : 2 * slab + 2, :] = limit[slab : slab + 1, :] - 1

    spread_limit(limit_out[...], 2)

    for t in range(clim_ref.shape[0] // 8):
        block = clim_ref[8 * t : 8 * t + 8, :]
        for k in range(8):
            for slab in range(slabs):
                row = 2 * slab + k % 2
                clim_rows[4 * t + k // 2, row : row + 1, :] = block[
                    k : k + 1, slab * LANES : (slab + 1) * LANES
                ]

    width = slabs * MODES
    depth = n_lev * rows
    levels = modes_ref.shape[1]
    q = lax.broadcasted_iota(jnp.int32, (depth, levels), 0)
    l = lax.broadcasted_iota(jnp.int32, (depth, levels), 1)
    spread_levels = jnp.where(2 * (q // rows) + lax.rem(q, 2) == l, 1.0, 0.0).astype(jnp.bfloat16)
    m = lax.broadcasted_iota(jnp.int32, (MODES, width), 0)
    r = lax.broadcasted_iota(jnp.int32, (MODES, width), 1)
    spread_modes = jnp.where(lax.rem(r, MODES) == m, 1.0, 0.0).astype(jnp.bfloat16)
    tall = lax.dot_general(
        spread_levels, modes_ref[...], (((1,), (1,)), ((), ())), preferred_element_type=jnp.float32
    ).astype(jnp.bfloat16)
    wide = jnp.dot(tall, spread_modes, preferred_element_type=jnp.float32)
    q = lax.broadcasted_iota(jnp.int32, (depth, width), 0)
    r = lax.broadcasted_iota(jnp.int32, (depth, width), 1)
    wide = jnp.where(r // MODES == lax.rem(q, rows) // 2, wide, 0.0)
    weights[...] = wide.astype(jnp.bfloat16)

    for s in range(n_lev):
        water_clim[s * rows : (s + 1) * rows] = jnp.where(limit_rows[2] > 2 * s, clim_rows[s], 0.0)
    source = q // rows
    dy = lax.rem(me_l // N_X + n_y - source // N_X, n_y)
    dx = lax.rem(lax.rem(me_l, N_X) + N_X - lax.rem(source, N_X), N_X)
    below = ((dy > 0) & (dy < reach)) | ((dy == reach) & (dx >= first_k))
    above = (dy > reach) | ((dy == reach) & (dx < first_k))
    q_copies = []
    for side, sign in enumerate(SIDES):
        q_out[side] = lax.dot_general(
            jnp.where(above if side else below, wide, 0.0), water_clim[...], (((0,), (0,)), ((), ())),
            precision=lax.Precision.HIGHEST, preferred_element_type=jnp.float32,
        )
        q_copies.append(neighbour_copy(q_out.at[side], q_in.at[side], q_sem.at[side], -sign))
        q_copies[-1].start()

    for part in range(1, PARTS):
        send_blocks(part)

    for slot, hops, dx, dy in routes:
        s = at(-hops, -dx)
        turned[slot * rows : (slot + 1) * rows] = weights[pl.ds(pl.multiple_of(s * rows, rows), rows)]

    for copy in limit_copies:
        copy.wait_recv()
    for side in range(2):
        spread_limit(limit_in[side], side)

    def use(part, slot, s, kind):
        water = limit_rows[kind] > 2 * s
        for d in range(part * part_days, (part + 1) * part_days):
            value = recv[slot, d].astype(jnp.float32)
            if kind == 2:
                value = value - clim_rows[s]
            anomaly[pl.ds(pl.multiple_of(slot * rows, rows), rows), d * LANES : (d + 1) * LANES] = jnp.where(
                water, value, 0.0
            ).astype(jnp.bfloat16)

    def project(first, count, part, parts):
        span = slice(first * rows, (first + count) * rows)
        lanes = DAYS // parts * LANES
        return lax.dot_general(
            turned[span], anomaly[span, part * lanes : (part + 1) * lanes], (((0,), (0,)), ((), ())),
            preferred_element_type=jnp.float32,
        )

    for _, copy in stay:
        copy.wait()
    at_home = [slot - own_slots - side * per_side for side, slot in enumerate(sorted(slot for slot, _ in stay)[1:])]
    sum_copies = []
    for part in range(PARTS):

        @pl.loop(0, per_side)
        def _(j):
            k = j + first_k
            hops, turn = reach - 1 - k // N_X, lax.rem(k, N_X)
            for side, sign in enumerate(SIDES):
                dx = turn if side == 0 else N_X - 1 - turn
                y = lax.rem(me_l // N_X + n_y - sign * hops, n_y)
                s = y * N_X + lax.rem(lax.rem(me_l, N_X) + N_X - dx, N_X)
                slot = own_slots + side * per_side + j

                @pl.when(j != at_home[side])
                def _():
                    block_copy(part, s, s, slot).wait_recv()

                use(part, slot, s, side)

        for side, sign in enumerate(SIDES):
            if part == 0:
                q_copies[side].wait_recv()
            total = project(own_slots + side * per_side, per_side, part, PARTS)
            for d in range(part_days):
                sums_out[side, part, d] = (
                    total[:, d * LANES : (d + 1) * LANES] - q_in[side]
                ).astype(jnp.bfloat16)
            sum_copies.append(
                neighbour_copy(sums_out.at[side, part], sums_in.at[side, part], t_sem.at[side, part], sign)
            )
            sum_copies[-1].start()

    for slot, hops, dx, dy in routes:
        if slot < own_slots:
            s = at(0, -dx)
            for part in range(PARTS):
                if dx:
                    block_copy(part, s, s, slot).wait_recv()
                use(part, slot, s, 2)
    coef = project(0, own_slots, 0, 1)
    for part in range(PARTS):
        for slot, hops, dx, dy in routes:
            if (hops, dx) != (0, 0):
                block_copy(part, at(dy, dx), at(hops, dx), slot).wait_send()
    for copy in limit_copies + q_copies:
        copy.wait_send()
    for part in range(PARTS):
        for copy in sum_copies[2 * part : 2 * part + 2]:
            copy.wait_recv()
        for d in range(part * part_days, (part + 1) * part_days):
            block = coef[:, d * LANES : (d + 1) * LANES]
            for side in range(2):
                block = block + sums_in[side, part, d % part_days].astype(jnp.float32)
            for slab in range(slabs):
                stacked_ref[d * MODES : (d + 1) * MODES, slab * LANES : (slab + 1) * LANES] = block[
                    slab * MODES : (slab + 1) * MODES
                ]
    for copy in sum_copies:
        copy.wait_send()

    half = stacked_ref.shape[0] // 2
    share = half // CORES
    long, short = half // n_lev, share // n_lev

    def gram_block(x, y):
        return lax.dot_general(
            x, y, (((1,), (1,)), ((), ())),
            precision=lax.Precision.HIGHEST, preferred_element_type=jnp.float32,
        )

    def pack(c, out):
        row, rest = pl.multiple_of(c * half, half), pl.multiple_of(half + c * share, share)
        first = gram_block(stacked_ref[:half], stacked_ref[pl.ds(row, half)])
        last = gram_block(stacked_ref[pl.ds(rest, share)], stacked_ref[half:])
        for i in range(n_lev):
            out[i, :long] = first[i * long : (i + 1) * long]
            out[i, long:] = last[i * short : (i + 1) * short]

    def pair_copy(src, dst, k):
        return pltpu.make_async_remote_copy(
            src_ref=src, dst_ref=dst, send_sem=p_sem.at[k, 0], recv_sem=p_sem.at[k, 1],
            device_id=partner, device_id_type=MESH,
        )

    pack(1 - core, theirs)
    to_pair = pair_copy(theirs, pair_buf, 0)
    to_pair.start()
    pack(core, packed)
    to_pair.wait()
    packed[...] = packed[...] + pair_buf[...]

    def scatter_copy(to, slot, k):
        return pltpu.make_async_remote_copy(
            src_ref=packed.at[to], dst_ref=rs_buf.at[slot],
            send_sem=r_send.at[k], recv_sem=r_recv.at[k],
            device_id=(me_g, to), device_id_type=MESH,
        )

    for o, peer in enumerate(peers):
        scatter_copy(peer, me_l, o).start()

    rs_buf[me_l] = packed[me_l]

    for o, s in enumerate(senders):
        scatter_copy(s, s, o).wait_recv()

    sum_buf[me_z] = jnp.sum(rs_buf[...], axis=0)

    def sum_copy(to, slot, k):
        return pltpu.make_async_remote_copy(
            src_ref=sum_buf.at[me_z], dst_ref=sum_buf.at[slot],
            send_sem=s_send.at[k], recv_sem=s_recv.at[k],
            device_id=(to * CORES + core, me_l), device_id_type=MESH,
        )

    for o in range(1, n_z):
        sum_copy(z_to(o), me_z, o).start()
    for o, peer in enumerate(peers):
        scatter_copy(peer, me_l, o).wait_send()
    for o in range(1, n_z):
        s = z_from(o)
        sum_copy(s, s, o).wait_recv()

    total_cols = clim_ref.shape[1] * n_grp * n_lev
    gather_buf[core, me_l] = jnp.sum(sum_buf[...], axis=0) * (1.0 / total_cols)

    def gather_copy(to, slot, k):
        return pltpu.make_async_remote_copy(
            src_ref=gather_buf.at[core, me_l], dst_ref=gather_buf.at[core, slot],
            send_sem=g_send.at[k], recv_sem=g_recv.at[k],
            device_id=(me_g, to), device_id_type=MESH,
        )

    for o, peer in enumerate(peers):
        gather_copy(peer, me_l, o).start()
    for o in range(1, n_z):
        sum_copy(z_to(o), me_z, o).wait_send()
    for o, s in enumerate(senders):
        gather_copy(s, s, o).wait_recv()

    to_pair = pair_copy(gather_buf.at[core], gather_buf.at[core], 1)
    to_pair.start()
    gram_ref[core] = gather_buf[core]
    for o, peer in enumerate(peers):
        gather_copy(peer, me_l, o).wait_send()
    to_pair.wait()
    gram_ref[1 - core] = gather_buf[1 - core]


def exchange(n_grp, n_lev, ocean, climatology, land_mask, bottom_index, modes):
    days, levels_dev, cols_grp = ocean.shape
    col_dev = climatology.shape[1]
    slabs = col_dev // LANES
    rows = levels_dev * slabs
    width = DAYS * MODES
    half = width // 2
    piece = (half + half // CORES) // n_lev
    tiles = cols_grp // LANES
    ocean = ocean.reshape(days, levels_dev, tiles, LANES).transpose(0, 2, 1, 3)
    ocean = ocean.reshape(days, tiles * levels_dev, LANES)
    vmem, hbm = pl.BlockSpec(memory_space=pltpu.VMEM), pl.BlockSpec(memory_space=pltpu.HBM)
    operands = (
        ocean, climatology,
        land_mask.reshape(slabs, LANES), bottom_index.reshape(slabs, LANES), modes,
    )
    operands = [pltpu.with_memory_space_constraint(x, pltpu.HBM) for x in operands]
    return pl.pallas_call(
        functools.partial(exchange_kernel, n_grp, n_lev),
        out_shape=(
            jax.ShapeDtypeStruct((width, col_dev), jnp.float32),
            jax.ShapeDtypeStruct((CORES, n_lev, piece, half), jnp.float32),
        ),
        in_specs=[hbm] * 5,
        out_specs=(vmem, vmem),
        scratch_shapes=[
            pltpu.VMEM(climatology.shape, jnp.float32),
            pltpu.VMEM((slabs, LANES), jnp.int32),
            pltpu.VMEM((slabs, LANES), jnp.int32),
            pltpu.VMEM(modes.shape, jnp.bfloat16),
            pltpu.VMEM((n_lev, days, rows, LANES), jnp.bfloat16),
            pltpu.VMEM((n_lev, rows, LANES), jnp.float32),
            pltpu.VMEM((3, rows, LANES), jnp.int32),
            pltpu.VMEM((n_lev * rows, slabs * MODES), jnp.bfloat16),
            pltpu.VMEM((n_lev * rows, slabs * MODES), jnp.bfloat16),
            pltpu.VMEM((n_lev * rows, days * LANES), jnp.bfloat16),
            pltpu.VMEM((n_lev * rows, LANES), jnp.float32),
            pltpu.VMEM((slabs, LANES), jnp.int32),
            pltpu.VMEM((2, slabs, LANES), jnp.int32),
            pltpu.VMEM((2, slabs * MODES, LANES), jnp.float32),
            pltpu.VMEM((2, slabs * MODES, LANES), jnp.float32),
            pltpu.VMEM((2, PARTS, days // PARTS, slabs * MODES, LANES), jnp.bfloat16),
            pltpu.VMEM((2, PARTS, days // PARTS, slabs * MODES, LANES), jnp.bfloat16),
            pltpu.VMEM((n_lev, piece, half), jnp.float32),
            pltpu.VMEM((n_lev, piece, half), jnp.float32),
            pltpu.VMEM((n_lev, piece, half), jnp.float32),
            pltpu.VMEM((n_lev, piece, half), jnp.float32),
            pltpu.VMEM((n_grp // CORES, piece, half), jnp.float32),
            pltpu.VMEM((CORES, n_lev, piece, half), jnp.float32),
            pltpu.SemaphoreType.DMA((4,)),
            pltpu.SemaphoreType.DMA((3,)),
            pltpu.SemaphoreType.DMA((PARTS, n_lev)),
            pltpu.SemaphoreType.DMA((PARTS, n_lev)),
            pltpu.SemaphoreType.DMA((2, 2)),
            pltpu.SemaphoreType.DMA((2, 2)),
            pltpu.SemaphoreType.DMA((2, PARTS, 2)),
            pltpu.SemaphoreType.DMA((2, 2)),
            pltpu.SemaphoreType.DMA((n_lev,)),
            pltpu.SemaphoreType.DMA((n_lev,)),
            pltpu.SemaphoreType.DMA((n_grp // CORES,)),
            pltpu.SemaphoreType.DMA((n_grp // CORES,)),
            pltpu.SemaphoreType.DMA((n_lev,)),
            pltpu.SemaphoreType.DMA((n_lev,)),
        ],
        compiler_params=pltpu.CompilerParams(
            collective_id=0, has_side_effects=True, vmem_limit_bytes=VMEM_BYTES
        ),
        name="exchange",
    )(*operands)


def mm(a, b, dims=((1,), (0,))):
    return lax.dot_general(a, b, (dims, ((), ())), precision=lax.Precision.HIGHEST, preferred_element_type=jnp.float32)


def eliminate(a):
    n = a.shape[0]
    w = 8
    lane = lax.broadcasted_iota(jnp.int32, (w, n), 1)
    sub = lax.broadcasted_iota(jnp.int32, (w, n), 0)
    rows = [a[w * h : w * h + w] for h in range(n // w)]

    def spread(x):
        return jnp.broadcast_to(x, (w, n))

    for g in range(n // w):
        at = g * w
        col = [spread(rows[g][:, at + k : at + k + 1]) for k in range(w)]
        row = rows[g]
        pivots, splats = [], []
        for k in range(w):
            inv = 1.0 / spread(col[k][k : k + 1])
            pivot = jnp.where(lane == at + k, inv, spread(row[k : k + 1]) * inv)
            pivots.append(jnp.where((lane > at + k) & (lane < at + w), 0.0, pivot))
            splats.append({j: spread(col[j][k : k + 1]) * inv for j in range(k + 1, w)})
            if k < w - 1:
                m = jnp.where(sub > k, col[k], 0.0)
                row = jnp.where((lane == at + k) & (sub > k), 0.0, row) - m * pivot
                for j in range(k + 1, w):
                    col[j] = col[j] - m * splats[k][j]
        rows[g] = row
        inside = (lane >= at) & (lane < at + w)
        for h in range(g + 1, n // w):
            c = [spread(rows[h][:, at + k : at + k + 1]) for k in range(w)]
            out = jnp.where(inside, 0.0, rows[h])
            for k in range(w):
                for j in range(k + 1, w):
                    c[j] = c[j] - c[k] * splats[k][j]
            for k in range(w):
                out = out - c[k] * pivots[k]
            rows[h] = out
    upper, inverse = [], []
    for h in range(n // w):
        at = sub + w * h
        scale = lax.rsqrt(spread(jnp.sum(jnp.where(lane == at, rows[h], 0.0), axis=1, keepdims=True)))
        upper.append(jnp.where(lane >= at, rows[h] * scale, 0.0))
        inverse.append(jnp.where(lane == at, scale, jnp.where(lane < at, rows[h] * scale, 0.0)))
    return jnp.concatenate(upper, axis=0), jnp.concatenate(inverse, axis=0)

def whiten_kernel(
    pieces, stacked_ref, factor_hbm, whitened_hbm,
    gram_ref, factor_ref, whitened_ref, sem,
):
    half = gram_ref.shape[1]
    long, short = half // pieces.shape[1], half // CORES // pieces.shape[1]
    first_out = pltpu.make_async_copy(whitened_ref.at[:half], whitened_hbm.at[:half], sem.at[0])
    cols = whitened_ref.shape[1] // 2
    second_out = [
        pltpu.make_async_copy(
            whitened_ref.at[half:, i * cols : (i + 1) * cols],
            whitened_hbm.at[half:, i * cols : (i + 1) * cols],
            sem.at[1 + i],
        )
        for i in range(2)
    ]
    factor_out = pltpu.make_async_copy(factor_ref, factor_hbm, sem.at[3])
    for c in range(CORES):
        for i in range(pieces.shape[1]):
            gram_ref[c, i * long : (i + 1) * long] = pieces[c, i, :long]
            at = c * (half // CORES) + i * short
            gram_ref[CORES, at : at + short] = pieces[c, i, long:]
    r11, i11 = eliminate(gram_ref[0])
    r12 = mm(i11, gram_ref[1])
    factor_ref[:half, :half] = r11
    factor_ref[:half, half:] = r12
    factor_ref[half:, :half] = jnp.zeros((half, half), jnp.float32)
    rest = gram_ref[2] - mm(r12, r12, ((0,), (0,)))
    first = mm(i11, stacked_ref[:half])
    whitened_ref[:half] = first
    first_out.start()
    left = stacked_ref[half:] - mm(r12, first, ((0,), (0,)))
    r22, i22 = eliminate(rest)
    factor_ref[half:, half:] = r22
    factor_out.start()
    for i in range(2):
        whitened_ref[half:, i * cols : (i + 1) * cols] = mm(i22, left[:, i * cols : (i + 1) * cols])
        second_out[i].start()
    first_out.wait()
    factor_out.wait()
    for i in range(2):
        second_out[i].wait()


def whiten(gram, stacked):
    vmem, hbm = pl.BlockSpec(memory_space=pltpu.VMEM), pl.BlockSpec(memory_space=pltpu.HBM)
    factor_shape = (stacked.shape[0],) * 2
    return pl.pallas_call(
        whiten_kernel,
        out_shape=(
            jax.ShapeDtypeStruct(factor_shape, jnp.float32),
            jax.ShapeDtypeStruct(stacked.shape, jnp.float32),
        ),
        in_specs=[vmem, vmem],
        out_specs=(hbm, hbm),
        scratch_shapes=[
            pltpu.VMEM((CORES + 1, gram.shape[3], gram.shape[3]), jnp.float32),
            pltpu.VMEM(factor_shape, jnp.float32),
            pltpu.VMEM(stacked.shape, jnp.float32),
            pltpu.SemaphoreType.DMA((4,)),
        ],
        compiler_params=pltpu.CompilerParams(vmem_limit_bytes=VMEM_BYTES),
        name="whiten",
    )(gram, stacked)


def solution(mesh):
    n_grp, n_lev = mesh.shape["grp"], mesh.shape["lev"]

    def on_device(ocean_field, climatology, land_mask, bottom_index, vertical_modes):
        stacked, gram = exchange(
            n_grp, n_lev, ocean_field, climatology, land_mask, bottom_index, vertical_modes
        )
        return whiten(gram, stacked)

    in_specs = (
        P(None, "lev", "grp"),
        P(None, ("grp", "lev")),
        P(("grp", "lev")),
        P(("grp", "lev")),
        P(),
    )
    out_specs = (P(), P(None, ("grp", "lev")))
    return jax.shard_map(
        on_device, mesh=mesh, in_specs=in_specs, out_specs=out_specs, check_vma=False
    )
```
